32 devices in a mesh: gz: 4 (over y, core), gy: 8 (over z, x).
Axes of the slice: x: 2, y: 2, z: 4, core: 2. Of those that a mesh axis runs over, the one named last changes fastest.
Arguments:
- image: bfloat16 [32, 16, 1024], P(('gz', 'gy')), may hold values from -8 to 8
- offsets: int32 [32, 2], P(('gz', 'gy')), may hold values from -32 to 32, as said below
- w_stem: bfloat16 [9, 32, 1], replicated, may hold values from -2 to 2
- b_stem: float32 [32], replicated, may hold values from -1.75 to 1.75
- w_skip: bfloat16 [9, 32, 32], replicated, may hold values from -0.375 to 0.375
- b_skip: float32 [32], replicated, may hold values from -1.75 to 1.75
- w_coarse: bfloat16 [27, 64, 32], replicated, may hold values from -0.21875 to 0.21875
- b_coarse: float32 [64], replicated, may hold values from -1.75 to 1.75
- w_lift: bfloat16 [32, 64], replicated, may hold values from -0.75 to 0.75
- b_lift: float32 [32], replicated, may hold values from -1.75 to 1.75
- w_final: bfloat16 [9, 32, 32], replicated, may hold values from -0.375 to 0.375
- b_final: float32 [32], replicated, may hold values from -1.75 to 1.75
- w_head: bfloat16 [3, 32], replicated, may hold values from -1 to 1
- b_head: float32 [3], replicated, may hold values from -3 to 3
Outputs:
- affinity: float32 [3, 32, 16, 1024], P(None, None, 'gy', 'gz')
The draws below stay inside these ranges and needn't reach their ends.
Inputs may be any that keep to these rules, and one draw needn't show every extreme that they name: offsets[s, 0] and offsets[s, 1] are section s's shifts along y and along x in pixels.
All inputs are finite; a program needn't handle non-finite values.
Results may differ from the reference program's by a relative error of at most 0.0054.
Values may be sent and summed in bfloat16 or wider, within the bound.
No kernel may reach another device: no remote copies, remote signals or barrier semaphores. Data moves between devices by JAX's collectives and lax.ppermute only.
A program may use at most 256 MiB of HBM per device.

```python
import jax
import jax.numpy as jnp
from jax import lax

BX = 256
C0 = 32
C1 = 64
OUTC = 3
MAXOFF = 32
Z = 32
Y = 16
X = 1024
N_GZ = 4


def draw_offsets(key, part):
    first, second = jax.random.split(jax.random.fold_in(key, 7))
    shifts = jax.random.randint(first, (Z, 2), -MAXOFF, MAXOFF + 1).astype(jnp.int32)
    chosen = jax.random.permutation(second, Z)
    shifts = shifts.at[chosen[0], 0].set(MAXOFF)
    shifts = shifts.at[chosen[1], 0].set(-MAXOFF)
    shifts = shifts.at[chosen[0], 1].set(-MAXOFF)
    shifts = shifts.at[chosen[1], 1].set(MAXOFF)
    return shifts


def block_scale(rng, extent, pieces, least, top_value):
    def one(axis_at, shards_of):
        steps = jax.random.uniform(jax.random.fold_in(jax.random.fold_in(rng, 6), axis_at), (shards_of,), jnp.float32, least / len(pieces), top_value / len(pieces))
        return jnp.repeat(jnp.exp(steps), extent[axis_at] // shards_of).reshape((-1,) + (1,) * (len(extent) - axis_at - 1))

    gain = one(*pieces[0])
    for cut in pieces[1:]:
        gain = gain * one(*cut)
    return gain


def gaussian(own_key, extent, scale, limit, shards=(), held_as=jnp.bfloat16):
    entries = jax.random.normal(own_key, extent, jnp.float32) * scale
    if len(shards) > 0:
        entries = block_scale(own_key, extent, shards, -0.22, 0.18) * entries
    return jnp.clip(entries, min=-limit, max=limit).astype(held_as)


def setup_inputs(seed: int = 0) -> dict:
    keys = jax.random.split(jax.random.key(seed), 15)
    return {
        "image": gaussian(keys[0], (Z, Y, X), 2.0, 8.0, ((0, 32),)),
        "offsets": draw_offsets(jax.random.fold_in(keys[14], 71), 0),
        "w_stem": gaussian(keys[2], (9, C0, 1), 9 ** -0.5, 2.0),
        "b_stem": gaussian(keys[3], (C0,), 0.3, 1.75, (), jnp.float32),
        "w_skip": gaussian(keys[4], (9, C0, C0), (9 * C0) ** -0.5, 0.375),
        "b_skip": gaussian(keys[5], (C0,), 0.3, 1.75, (), jnp.float32),
        "w_coarse": gaussian(keys[6], (27, C1, C0), (27 * C0) ** -0.5, 0.21875),
        "b_coarse": gaussian(keys[7], (C1,), 0.3, 1.75, (), jnp.float32),
        "w_lift": gaussian(keys[8], (C0, C1), C1 ** -0.5, 0.75),
        "b_lift": gaussian(keys[9], (C0,), 0.3, 1.75, (), jnp.float32),
        "w_final": gaussian(keys[10], (9, C0, C0), (9 * C0) ** -0.5, 0.375),
        "b_final": gaussian(keys[11], (C0,), 0.3, 1.75, (), jnp.float32),
        "w_head": gaussian(keys[12], (OUTC, C0), C0 ** -0.5, 1.0),
        "b_head": gaussian(keys[13], (OUTC,), 0.5, 3.0, (), jnp.float32),
    }


def shift_sections(image, offsets):
    full_y = image.shape[1]
    full_x = image.shape[2]
    padded = jnp.pad(image, ((0, 0), (MAXOFF, MAXOFF), (MAXOFF, MAXOFF)))

    def place(section, offset):
        return lax.dynamic_slice(section, ((MAXOFF - offset[0]).astype(jnp.int32), (MAXOFF - offset[1]).astype(jnp.int32)), (full_y, full_x))

    return jax.vmap(place)(padded, offsets)


def lateral_conv(padded, weight):
    out_y = padded.shape[2] - 2
    out_x = padded.shape[3] - 2
    total = jnp.zeros((weight.shape[1], padded.shape[1], out_y, out_x), jnp.float32)
    for tap_y in range(3):
        for tap_x in range(3):
            window = padded[:, :, tap_y:tap_y + out_y, tap_x:tap_x + out_x].astype(jnp.float32)
            total = total + jnp.einsum("oc,czyx->ozyx", weight[tap_y * 3 + tap_x].astype(jnp.float32), window)
    return total


def volume_conv(padded, weight):
    out_z = padded.shape[1] - 2
    out_y = padded.shape[2] - 2
    out_x = padded.shape[3] - 2
    total = jnp.zeros((weight.shape[1], out_z, out_y, out_x), jnp.float32)
    for tap_z in range(3):
        for tap_y in range(3):
            for tap_x in range(3):
                window = padded[:, tap_z:tap_z + out_z, tap_y:tap_y + out_y, tap_x:tap_x + out_x].astype(jnp.float32)
                total = total + jnp.einsum("oc,czyx->ozyx", weight[tap_z * 9 + tap_y * 3 + tap_x].astype(jnp.float32), window)
    return total


def inside_mask(row_start, col_start, rows, cols, full_y, full_x):
    row_pos = row_start + jnp.arange(rows, dtype=jnp.int32)
    col_pos = col_start + jnp.arange(cols, dtype=jnp.int32)
    row_in = (row_pos >= 0) & (row_pos < full_y)
    col_in = (col_pos >= 0) & (col_pos < full_x)
    return (row_in[:, None] & col_in[None, :]).astype(jnp.float32)[None, None]


def column4(bias):
    return bias.astype(jnp.float32)[:, None, None, None]


def reference(image, offsets, w_stem, b_stem, w_skip, b_skip, w_coarse, b_coarse, w_lift, b_lift, w_final, b_final, w_head, b_head):
    shifted = shift_sections(image, offsets)
    volume_padded = jnp.pad(shifted, ((0, 0), (8, 8), (8, 8)))

    def strip(index):
        col_start = index * BX
        region = lax.dynamic_slice_in_dim(volume_padded, col_start, BX + 16, 2)
        stem = lateral_conv(region[None], w_stem)
        stem_map = (jax.nn.relu(stem + column4(b_stem)) * inside_mask(-7, col_start - 7, Y + 14, BX + 14, Y, X)).astype(jnp.bfloat16)
        skip = lateral_conv(stem_map, w_skip)
        skip_map = (jax.nn.relu(skip + column4(b_skip)) * inside_mask(-6, col_start - 6, Y + 12, BX + 12, Y, X)).astype(jnp.bfloat16)
        pooled = skip_map.reshape(C0, Z, (Y + 12) // 2, 2, (BX + 12) // 2, 2).max(axis=(3, 5))
        coarse = volume_conv(jnp.pad(pooled, ((0, 0), (1, 1), (0, 0), (0, 0))), w_coarse)
        coarse_map = jax.nn.relu(coarse + column4(b_coarse)).astype(jnp.bfloat16)
        lifted = jnp.einsum("oc,czyx->ozyx", w_lift.astype(jnp.float32), coarse_map.astype(jnp.float32))
        lifted = jnp.repeat(jnp.repeat(lifted, 2, axis=2), 2, axis=3)
        merged = jax.nn.relu(skip_map[:, :, 2:-2, 2:-2].astype(jnp.float32) + lifted + column4(b_lift))
        merged = (merged * inside_mask(-4, col_start - 4, Y + 8, BX + 8, Y, X)).astype(jnp.bfloat16)
        final = lateral_conv(merged, w_final)
        final_map = jax.nn.relu(final + column4(b_final))[:, :, 3:-3, 3:-3].astype(jnp.bfloat16)
        logits = jnp.einsum("oc,czyx->ozyx", w_head.astype(jnp.float32), final_map.astype(jnp.float32))
        return logits + column4(b_head)

    strips = lax.map(strip, jnp.arange(N_GZ, dtype=jnp.int32))
    return strips.transpose(1, 2, 3, 0, 4).reshape(OUTC, Z, Y, X)
```

```python
import functools

import jax
import jax.numpy as jnp
from jax import lax
from jax.experimental import pallas as pl
from jax.experimental.pallas import tpu as pltpu
from jax.sharding import PartitionSpec as P

MAXOFF = 32
HALO = 8
SLOTS = 16
HALO_Y = 7
LANES = 128
PAD = MAXOFF + HALO
BF16, F32, I32 = jnp.bfloat16, jnp.float32, jnp.int32
VMEM_BYTES = 58 * 1024 * 1024


def iota(shape, dim):
    return lax.broadcasted_iota(I32, shape, dim)


def dot(a, b):
    return jnp.dot(a, b, preferred_element_type=F32)


def dot_tn(a, b):
    return lax.dot_general(a, b, (((0,), (0,)), ((), ())), preferred_element_type=F32)


def dot_nt(a, b):
    return lax.dot_general(a, b, (((1,), (1,)), ((), ())), preferred_element_type=F32)


def relu(x):
    return jnp.maximum(x, 0.0)


def round_up(n, m):
    return -(-n // m) * m


def divisor(count, most):
    return max(d for d in range(1, count + 1) if count % d == 0 and d <= max(most, 1))


def send_kernel(parts_gz, parts_gy, brick_y, brick_x, off_ref, image_ref, send_ref, tall_ref):
    full_y, full_x = image_ref.shape[1:]
    blocks = full_x // 8 + 2
    rows = round_up(blocks, 8)
    mine = brick_x // 8 + 2
    off_y, off_x = off_ref[0, 0], off_ref[0, 1]
    tall_ref[...] = jnp.zeros_like(tall_ref)
    tall_ref[PAD : PAD + full_x, 0:full_y] = image_ref[0].astype(F32).T
    lane, block = iota((rows, LANES), 1), iota((rows, LANES), 0)
    in_section = (block >= 1) & (block < blocks - 1)
    halves = full_y // SLOTS
    packed = [jnp.zeros((rows, LANES), F32) for _ in range(halves)]
    for i in range(8):
        column = tall_ref[pl.ds(PAD - HALO + i - off_x, rows, stride=8), :]
        for h in range(halves):
            turn = lax.rem(off_y + (16 * i - 16 * h + 2 * LANES), LANES)
            turned = pltpu.roll(column, turn, axis=1)
            packed[h] = jnp.where(((lane >> 4) == i) & in_section, turned, packed[h])
    slot = lane & 15
    for gy in range(parts_gy):
        start = brick_y * gy - HALO_Y
        window = jnp.zeros((rows, LANES), F32)
        for h in range(halves):
            shift = start - 16 * h
            if -16 < shift < 16:
                turned = pltpu.roll(packed[h], (-shift) % LANES, axis=1)
                inside = (slot + shift >= 0) & (slot + shift < 16)
                window = jnp.where(inside, turned, window)
        for gz in range(parts_gz):
            first = gz * (brick_x // 8)
            send_ref[gz * parts_gy + gy] = window[first : first + mine].astype(BF16)


def make_windows(image, offsets, parts_gz, parts_gy):
    full_y, full_x = image.shape[1:]
    brick_y, brick_x = full_y // parts_gy, full_x // parts_gz
    rows = round_up(full_x // 8 + 2, 8)
    tall = round_up(PAD - HALO + 7 + MAXOFF + 8 * (rows - 1) + 1, 8)
    return pl.pallas_call(
        functools.partial(send_kernel, parts_gz, parts_gy, brick_y, brick_x),
        out_shape=jax.ShapeDtypeStruct((parts_gz * parts_gy, brick_x // 8 + 2, LANES), BF16),
        in_specs=[
            pl.BlockSpec(memory_space=pltpu.SMEM),
            pl.BlockSpec(memory_space=pltpu.VMEM),
        ],
        out_specs=pl.BlockSpec(memory_space=pltpu.VMEM),
        scratch_shapes=[pltpu.VMEM((tall, LANES), F32)],
    )(offsets, image)


def stem_row(s):
    return jnp.where(s < 8, s + 2, jnp.where(s < 12, s - 8, s - 4))


def within(y, full_y):
    return (y >= 0) & (y < full_y)


def prep_kernel(
    brick_y,
    full_y,
    pos_ref,
    w_stem,
    w_skip,
    w_coarse,
    w_lift,
    w_final,
    w_head,
    b4,
    b_coarse,
    ws,
    wa,
    wb,
    wc,
    wl,
    wf,
    wh,
    bias,
):
    y0 = pos_ref[1] * brick_y
    zero = jnp.zeros((32, 256), F32)

    def tiles(count, width):
        return jnp.where((iota((count, width), 1) & (count - 1)) == iota((count, width), 0), 1.0, 0.0)

    t512_f, t256_f, t64_f = tiles(32, 512), tiles(32, 256), tiles(64, 256)
    t512, t256, t64 = t512_f.astype(BF16), t256_f.astype(BF16), t64_f.astype(BF16)

    def spread(row, table):
        return jnp.dot(row, table, precision=lax.Precision.HIGHEST, preferred_element_type=F32)

    lane = iota((1, 512), 1)
    t_of = stem_row(lane >> 5)
    stem_ok = within(y0 - 5 + t_of, full_y)
    rep = dot(w_stem[...], t512)
    lane16 = iota((16, 512), 1)
    t16 = stem_row(lane16 >> 5)
    tap16 = iota((16, 512), 0) - t16 - 1
    ok16 = within(y0 - 5 + t16, full_y)
    ws[...] = jnp.zeros_like(ws)
    for dx in range(3):
        block = jnp.zeros((16, 512), F32)
        for a in range(3):
            block = jnp.where((tap16 == a) & ok16, rep[3 * a + dx : 3 * a + dx + 1], block)
        ws[112 + 16 * dx : 128 + 16 * dx] = block.astype(BF16)
    bias[...] = jnp.zeros_like(bias)
    bias[0:1] = jnp.where(stem_ok, spread(b4[0:1], t512_f), 0.0)

    lane = iota((32, 256), 1)
    half, quarter = lane >> 7, (lane >> 5) & 3
    row_a = 2 + 2 * quarter + half
    ok_a = (quarter < 3) & within(y0 - 4 + row_a, full_y)
    row_a = jnp.where(ok_a, row_a, -99)
    xpar = quarter >> 1
    row_b = 8 * (quarter & 1) + half
    ok_b = within(y0 - 4 + row_b, full_y)
    row_b = jnp.where(ok_b, row_b, -99)
    reps = [dot_tn(w_skip[tap], t256) for tap in range(9)]
    for dx in range(3):
        for i in range(8):
            block = zero
            for a in range(3):
                block = jnp.where(row_a == 2 + i - a, reps[3 * a + dx], block)
            wa[256 * dx + 32 * i : 256 * dx + 32 * i + 32] = block.astype(BF16)
    for j in range(4):
        for i in range(8):
            t = i if i < 4 else i + 4
            block = zero
            for a in range(3):
                for p in range(2):
                    if 0 <= j - p < 3:
                        block = jnp.where(
                            (row_b == t - a) & (xpar == p), reps[3 * a + j - p], block
                        )
            wb[256 * j + 32 * i : 256 * j + 32 * i + 32] = block.astype(BF16)
    b_skip = spread(b4[1:2], t256_f)
    bias[1:2, 0:256] = jnp.where(ok_a[0:1], b_skip, 0.0)
    bias[2:3, 0:256] = jnp.where(ok_b[0:1], b_skip, 0.0)

    slots = []
    for c in range(3):
        slots += [(1, c), (2, c), (3, c), ((None, 0), (0, 2), (4, 2))[c]]
    slots += [(0, 0), (4, 0), (0, 1), (4, 1)]
    q_of = lane >> 6
    for dx in range(3):
        reps = [dot_tn(w_coarse[3 * ca + dx], t64) for ca in range(9)]
        for i, (p, c) in enumerate(slots):
            block = zero
            if p is not None:
                for a in range(3):
                    block = jnp.where(q_of == p - a, reps[3 * c + a], block)
            wc[512 * dx + 32 * i : 512 * dx + 32 * i + 32] = block.astype(BF16)
    bias[3:4, 0:256] = spread(b_coarse[...], t64_f)

    lane64 = iota((64, 256), 1)
    quarter64 = (lane64 >> 5) & 3
    ok64 = within(y0 - 2 + 2 * quarter64 + (lane64 >> 7), full_y)
    rep = dot_tn(w_lift[...], t256)
    for q in range(3):
        wl[64 * q : 64 * q + 64] = jnp.where((quarter64 == q) & ok64, rep, 0.0).astype(BF16)
    wl[192:256] = jnp.zeros((64, 256), BF16)
    bias[4:5, 0:256] = jnp.where(ok_a[0:1], spread(b4[2:3], t256_f), 0.0)

    xi_of, f_of = lane >> 6, (lane >> 5) & 1
    reps = [dot_tn(w_final[tap], t256) for tap in range(9)]
    for j in range(6):
        for i in range(8):
            row = 2 + 2 * (i & 3) + (i >> 2)
            block = zero
            if (i & 3) < 3:
                for a in range(3):
                    for dx in range(3):
                        if 0 <= row - 3 - a < 2 and 0 <= j - dx < 4:
                            block = jnp.where(
                                (f_of == row - 3 - a) & (xi_of == j - dx), reps[3 * a + dx], block
                            )
            wf[256 * j + 32 * i : 256 * j + 32 * i + 32] = block.astype(BF16)
    bias[5:6, 0:256] = spread(b4[3:4], t256_f)

    row = iota((32, 256), 0)
    rep = dot(w_head[...], t256)
    block = zero
    for o in range(3):
        here = ((row >> 3) == xi_of) & ((row & 7) == 2 * o + f_of)
        block = jnp.where(here, rep[o : o + 1], block)
    wh[...] = block.astype(BF16)


def prepare(pos, brick_y, full_y, w_stem, w_skip, w_coarse, w_lift, w_final, w_head, b4, b_coarse):
    shapes = [(272, 512), (768, 256), (1024, 256), (1536, 256), (256, 256), (1536, 256), (32, 256)]
    vmem = pl.BlockSpec(memory_space=pltpu.VMEM)
    return pl.pallas_call(
        functools.partial(prep_kernel, brick_y, full_y),
        out_shape=[jax.ShapeDtypeStruct(s, BF16) for s in shapes]
        + [jax.ShapeDtypeStruct((8, 512), F32)],
        in_specs=[pl.BlockSpec(memory_space=pltpu.SMEM)] + [vmem] * 8,
        out_specs=[vmem] * 8,
        cost_estimate=pl.CostEstimate(
            flops=100_000_000, bytes_accessed=4_000_000, transcendentals=0
        ),
        compiler_params=pltpu.CompilerParams(vmem_limit_bytes=VMEM_BYTES),
    )(pos, w_stem, w_skip, w_coarse, w_lift, w_final, w_head, b4, b_coarse)


def brick_kernel(
    parts_gz,
    cols,
    steps,
    pos_ref,
    b_head,
    r_ref,
    ws,
    wa,
    wb,
    wc,
    wl,
    wf,
    wh,
    bias,
    out_ref,
    tmp,
    rin,
    stem,
    skip,
    pooled,
    fin,
):
    nz, have = r_ref.shape[0:2]
    pitch = tmp.shape[0] // nz
    blocks = cols // 8 + 2
    step = 0 if steps == 1 else pl.program_id(0)
    leftmost = (pos_ref[0] == 0) & (step == 0)
    rightmost = (pos_ref[0] == parts_gz - 1) & (step == steps - 1)

    for z in range(nz):
        tmp[z * pitch : z * pitch + have] = r_ref[z].astype(F32)
    for b in range(blocks):
        rin[b] = tmp[pl.ds(step * (cols // 8) + b, nz, stride=pitch), :].astype(BF16)

    b_stem = bias[0:1, :]

    def stem_put(acc, first, i):
        out = relu(acc + b_stem).astype(BF16)
        for b in range(acc.shape[0] // nz):
            stem[4 * (first + b) + (i >> 1), i & 1] = out[b * nz : b * nz + nz]

    def stem_mid(i, carry):
        start = pl.multiple_of(128 - 16 * i, 16)
        weight = ws[pl.ds(start, LANES), :]
        stem_put(dot(rin[...].reshape(blocks * nz, LANES), weight), 0, i)
        return carry

    lax.fori_loop(1, 7, stem_mid, 0)
    pair = jnp.concatenate([rin[0 : blocks - 1], rin[1:blocks]], axis=-1)
    pair = pair.reshape((blocks - 1) * nz, 2 * LANES)
    stem_put(dot(pair, ws[0:256]), 1, 0)
    stem_put(dot(pair, ws[16:272]), 0, 7)

    @pl.when(leftmost)
    def _():
        stem[0:4] = jnp.zeros((4,) + stem.shape[1:], BF16)

    @pl.when(rightmost)
    def _():
        stem[4 * blocks - 4 : 4 * blocks] = jnp.zeros((4,) + stem.shape[1:], BF16)

    pairs = cols // 2 + 4
    mc = divisor(pairs, 512 // nz)
    m_rows = mc * nz

    def skip_step(i, carry):
        m0 = i * mc

        def taken(u, half):
            part = stem[pl.ds(m0 + u // 2, mc), u % 2, :, 256 * half : 256 * half + 256]
            return part.reshape(m_rows, 256)

        top = None
        for p in range(2):
            acc = dot(taken(3 + p, 0), wa[0:256])
            acc += dot(taken(4 + p, 0), wa[256:512])
            acc += dot(taken(5 + p, 0), wa[512:768])
            acc = relu(acc + bias[1:2, 0:256])
            skip[pl.ds(m0, mc), p] = acc.astype(BF16).reshape(mc, nz, 256)
            best = jnp.maximum(acc[:, 0:128], acc[:, 128:256])
            top = best if top is None else jnp.maximum(top, best)
        acc = dot(taken(3, 1), wb[0:256])
        for j in range(1, 4):
            acc += dot(taken(3 + j, 1), wb[256 * j : 256 * j + 256])
        best = jnp.maximum(acc[:, 0:128], acc[:, 128:256])
        best = jnp.maximum(best, pltpu.roll(best, 64, axis=1))
        ends = relu(best + bias[2:3, 0:128])
        z_of = iota((mc, nz, LANES), 1).reshape(m_rows, LANES)
        lane = iota((m_rows, LANES), 1)
        bottom, summit = z_of == 0, z_of == nz - 1

        def below(x):
            return jnp.where(bottom, 0.0, pltpu.roll(x, 1, axis=0))

        def above(x):
            return jnp.where(summit, 0.0, pltpu.roll(x, m_rows - 1, axis=0))

        ends_above = above(ends)
        parts = (
            below(top),
            jnp.where(lane < 96, top, pltpu.roll(ends_above, 32, axis=1)),
            jnp.where(lane < 96, above(top), ends_above),
            jnp.where(lane < 64, below(ends), ends),
        )
        for k in range(4):
            pooled[pl.ds(m0, mc), :, 128 * k : 128 * k + 128] = (
                parts[k].astype(BF16).reshape(mc, nz, LANES)
            )
        return carry

    lax.fori_loop(0, pairs // mc, skip_step, 0)

    @pl.when(leftmost)
    def _():
        pooled[0:2] = jnp.zeros((2,) + pooled.shape[1:], BF16)

    @pl.when(rightmost)
    def _():
        pooled[pairs - 2 : pairs] = jnp.zeros((2,) + pooled.shape[1:], BF16)

    count = cols // 2 + 2
    nc = divisor(count, 512 // nz)
    n_rows = nc * nz

    def coarse_step(i, carry):
        n0 = i * nc
        acc = dot(pooled[pl.ds(n0, nc)].reshape(n_rows, 512), wc[0:512])
        acc += dot(pooled[pl.ds(n0 + 1, nc)].reshape(n_rows, 512), wc[512:1024])
        acc += dot(pooled[pl.ds(n0 + 2, nc)].reshape(n_rows, 512), wc[1024:1536])
        coarse = relu(acc + bias[3:4, 0:256]).astype(BF16)
        lifted = dot(coarse, wl[...])
        for p in range(2):
            base = skip[pl.ds(n0 + 1, nc), p].reshape(n_rows, 256).astype(F32)
            out = relu(base + lifted + bias[4:5, 0:256]).astype(BF16)
            for k in range(nc):
                n = n0 + k
                stem[n >> 1, n & 1, :, 256 * p : 256 * p + 256] = out[k * nz : k * nz + nz]
        return carry

    lax.fori_loop(0, count // nc, coarse_step, 0)

    @pl.when(leftmost)
    def _():
        stem[0, 0] = jnp.zeros(stem.shape[2:], BF16)

    @pl.when(rightmost)
    def _():
        stem[cols // 4, 1] = jnp.zeros(stem.shape[2:], BF16)

    quads = cols // 4
    qc = divisor(quads, 512 // nz)
    q_rows = qc * nz

    def final_step(i, carry):
        q0 = i * qc
        acc = jnp.zeros((q_rows, 256), F32)
        for j in range(6):
            k = (1 + j) % 4
            half = 256 * (k % 2)
            part = stem[pl.ds(q0 + (1 + j) // 4, qc), k // 2, :, half : half + 256]
            acc += dot(part.reshape(q_rows, 256), wf[256 * j : 256 * j + 256])
        out = relu(acc + bias[5:6, 0:256])
        for k in range(2):
            fin[k, pl.ds(pl.multiple_of(q0 * nz, 8), q_rows), :] = out[:, 128 * k : 128 * k + 128]
        return carry

    lax.fori_loop(0, quads // qc, final_step, 0)

    together = LANES // quads
    groups = nz // together
    lines = []
    for g in range(groups):
        sides = []
        for side in range(2):
            rows = [
                fin[side, pl.ds(g * together + k, quads, stride=nz), :] for k in range(together)
            ]
            sides.append(jnp.concatenate(rows, axis=0).astype(BF16))
        h = dot_nt(wh[...], jnp.concatenate(sides, axis=1))
        lines.append(jnp.concatenate([h[8 * xi : 8 * xi + 8] for xi in range(4)], axis=1))
    table = jnp.concatenate(lines, axis=0)
    size = together * cols
    row = iota((512, size), 0)
    order = jnp.where(iota((512, size), 1) == 4 * (row & 127) + (row >> 7), 1.0, 0.0).astype(BF16)
    high = table.astype(BF16)
    rest = table - high.astype(F32)
    middle = rest.astype(BF16)
    low = (rest - middle.astype(F32)).astype(BF16)
    result = dot(high, order) + (dot(middle, order) + dot(low, order))
    for g in range(groups):
        for k in range(together):
            for o in range(3):
                out_ref[o, g * together + k] = (
                    result[8 * g + 2 * o : 8 * g + 2 * o + 2, k * cols : k * cols + cols]
                    + b_head[o]
                )


def brick(pos, b_head, received, weights, parts_gz, brick_y, brick_x):
    nz, have = received.shape[0:2]
    cols = brick_x
    while cols * nz > 16384 and cols % 256 == 0:
        cols //= 2
    steps = brick_x // cols
    vmem = pl.BlockSpec(memory_space=pltpu.VMEM)
    smem = pl.BlockSpec(memory_space=pltpu.SMEM)
    return pl.pallas_call(
        functools.partial(brick_kernel, parts_gz, cols, steps),
        grid=(steps,),
        out_shape=jax.ShapeDtypeStruct((3, nz, brick_y, brick_x), F32),
        in_specs=[smem, smem] + [vmem] * 9,
        out_specs=pl.BlockSpec((3, nz, brick_y, cols), lambda i: (0, 0, 0, i)),
        scratch_shapes=[
            pltpu.VMEM((nz * round_up(have, 8), LANES), F32),
            pltpu.VMEM((cols // 8 + 2, nz, LANES), BF16),
            pltpu.VMEM((cols // 2 + 8, 2, nz, 512), BF16),
            pltpu.VMEM((cols // 2 + 4, 2, nz, 256), BF16),
            pltpu.VMEM((cols // 2 + 4, nz, 512), BF16),
            pltpu.VMEM((2, cols // 4 * nz, LANES), F32),
        ],
        cost_estimate=pl.CostEstimate(
            flops=20_000_000_000, bytes_accessed=4_000_000, transcendentals=0
        ),
        compiler_params=pltpu.CompilerParams(vmem_limit_bytes=VMEM_BYTES),
    )(pos, b_head, received, *weights)


def local(
    image,
    offsets,
    w_stem,
    b_stem,
    w_skip,
    b_skip,
    w_coarse,
    b_coarse,
    w_lift,
    b_lift,
    w_final,
    b_final,
    w_head,
    b_head,
):
    parts_gz, parts_gy = lax.axis_size("gz"), lax.axis_size("gy")
    full_y, full_x = image.shape[1:]
    brick_y, brick_x = full_y // parts_gy, full_x // parts_gz
    assert image.shape[0] == 1 and brick_y == 2
    pos = jnp.stack([lax.axis_index("gz"), lax.axis_index("gy")]).astype(I32)
    windows = make_windows(image, offsets, parts_gz, parts_gy)
    received = lax.all_to_all(windows, ("gz", "gy"), 0, 0, tiled=True)
    b4 = jnp.stack([b_stem, b_skip, b_lift, b_final])
    weights = prepare(
        pos,
        brick_y,
        full_y,
        w_stem.reshape(w_stem.shape[0:2]),
        w_skip,
        w_coarse,
        w_lift,
        w_final,
        w_head,
        b4,
        b_coarse[None],
    )
    return brick(pos, b_head, received, weights, parts_gz, brick_y, brick_x)


def solution(mesh):
    split = P(("gz", "gy"))
    return jax.shard_map(
        local,
        mesh=mesh,
        in_specs=(split, split) + (P(),) * 12,
        out_specs=P(None, None, "gy", "gz"),
        check_vma=False,
    )
```

```python
import functools
import math

import jax
import jax.numpy as jnp
from jax import lax
from jax.experimental import pallas as pl
from jax.experimental.pallas import tpu as pltpu
from jax.sharding import PartitionSpec as P

MAXOFF = 32
HALO = 8
SLOTS = 16
HALO_Y = 7
LANES = 128
PAD = MAXOFF + HALO
BF16, F32, I32 = jnp.bfloat16, jnp.float32, jnp.int32
MIB = 1024 * 1024


def iota(shape, dim):
    return lax.broadcasted_iota(I32, shape, dim)


def dot(a, b):
    return jnp.dot(a, b, preferred_element_type=F32)


def dot_tn(a, b):
    return lax.dot_general(a, b, (((0,), (0,)), ((), ())), preferred_element_type=F32)


def dot_nt(a, b):
    return lax.dot_general(a, b, (((1,), (1,)), ((), ())), preferred_element_type=F32)


def relu(x):
    return jnp.maximum(x, 0.0)


def round_up(n, m):
    return -(-n // m) * m


def divisor(count, most):
    return max(d for d in range(1, count + 1) if count % d == 0 and d <= max(most, 1))


def send_kernel(parts_gz, parts_gy, brick_y, brick_x, off_ref, image_ref, send_ref, tall_ref):
    full_y, full_x = image_ref.shape[1:]
    blocks = full_x // 8 + 2
    rows = round_up(blocks, 8)
    mine = brick_x // 8 + 2
    off_y, off_x = off_ref[0, 0], off_ref[0, 1]
    tall_ref[...] = jnp.zeros_like(tall_ref)
    tall_ref[PAD : PAD + full_x, 0:full_y] = image_ref[0].astype(F32).T
    lane, block = iota((rows, LANES), 1), iota((rows, LANES), 0)
    in_section = (block >= 1) & (block < blocks - 1)
    halves = full_y // SLOTS
    packed = [jnp.zeros((rows, LANES), F32) for _ in range(halves)]
    for i in range(8):
        column = tall_ref[pl.ds(PAD - HALO + i - off_x, rows, stride=8), :]
        for h in range(halves):
            turn = lax.rem(off_y + (16 * i - 16 * h + 2 * LANES), LANES)
            turned = pltpu.roll(column, turn, axis=1)
            packed[h] = jnp.where(((lane >> 4) == i) & in_section, turned, packed[h])
    slot = lane & 15
    for gy in range(parts_gy):
        start = brick_y * gy - HALO_Y
        window = jnp.zeros((rows, LANES), F32)
        for h in range(halves):
            shift = start - 16 * h
            if -16 < shift < 16:
                turned = pltpu.roll(packed[h], (-shift) % LANES, axis=1)
                inside = (slot + shift >= 0) & (slot + shift < 16)
                window = jnp.where(inside, turned, window)
        for gz in range(parts_gz):
            first = gz * (brick_x // 8)
            send_ref[gz * parts_gy + gy] = window[first : first + mine].astype(BF16)


def make_windows(image, offsets, parts_gz, parts_gy):
    full_y, full_x = image.shape[1:]
    brick_y, brick_x = full_y // parts_gy, full_x // parts_gz
    rows = round_up(full_x // 8 + 2, 8)
    tall = round_up(PAD - HALO + 7 + MAXOFF + 8 * (rows - 1) + 1, 8)
    return pl.pallas_call(
        functools.partial(send_kernel, parts_gz, parts_gy, brick_y, brick_x),
        out_shape=jax.ShapeDtypeStruct((parts_gz * parts_gy, brick_x // 8 + 2, LANES), BF16),
        in_specs=[
            pl.BlockSpec(memory_space=pltpu.SMEM),
            pl.BlockSpec(memory_space=pltpu.VMEM),
        ],
        out_specs=pl.BlockSpec(memory_space=pltpu.VMEM),
        scratch_shapes=[pltpu.VMEM((tall, LANES), F32)],
    )(offsets, image)


ENDS = (0, 1, 10, 11, 2, 3, 8, 9)


SIZES = {"a": 768, "b": 1024, "c": 1536, "l": 256, "f": 1536, "h": 32, "s": 272, "t": 272, "v": 96}
STARTS = dict(zip(SIZES, [sum(list(SIZES.values())[:k]) for k in range(len(SIZES))]))
WEIGHT_ROWS = sum(SIZES.values())


def parts_of(ref):
    return [ref.at[STARTS[k] : STARTS[k] + SIZES[k]] for k in SIZES]


def in_three(x):
    high = x.astype(BF16)
    rest = x - high.astype(F32)
    middle = rest.astype(BF16)
    return high, middle, (rest - middle.astype(F32)).astype(BF16)


def stem_row(s):
    return jnp.where(s < 8, s + 2, jnp.where(s < 10, s - 8, s))


def within(y, full_y):
    return (y >= 0) & (y < full_y)


def prep_kernel(
    brick_y,
    full_y,
    pos_ref,
    b_head,
    w_stem,
    w_skip,
    w_coarse,
    w_lift,
    w_final,
    w_head,
    b4,
    b_coarse,
    packed,
    bias,
):
    wa, wb, wc, wl, wf, wh, ws, wt, wv = parts_of(packed)
    y0 = pos_ref[1] * brick_y
    zero = jnp.zeros((32, 256), F32)

    def tiles(count, width):
        return jnp.where((iota((count, width), 1) & (count - 1)) == iota((count, width), 0), 1.0, 0.0)

    t384_f, t256_f, t64_f = tiles(32, 384), tiles(32, 256), tiles(64, 256)
    t384, t256, t64 = t384_f.astype(BF16), t256_f.astype(BF16), t64_f.astype(BF16)

    def spread(row, table):
        return jnp.dot(row, table, precision=lax.Precision.HIGHEST, preferred_element_type=F32)

    lane = iota((1, 384), 1)
    t_of = stem_row(lane >> 5)
    stem_ok = within(y0 - 5 + t_of, full_y)
    rep = dot(w_stem[...], t384)
    lane16 = iota((16, 384), 1)
    t16 = stem_row(lane16 >> 5)
    tap16 = iota((16, 384), 0) - t16 - 1
    ok16 = within(y0 - 5 + t16, full_y)
    ws[...] = jnp.zeros((272, 256), BF16)
    wt[...] = jnp.zeros((272, 256), BF16)
    for dx in range(3):
        block = jnp.zeros((16, 384), F32)
        for a in range(3):
            block = jnp.where((tap16 == a) & ok16, rep[3 * a + dx : 3 * a + dx + 1], block)
        block = block.astype(BF16)
        ws[112 + 16 * dx : 128 + 16 * dx] = block[:, 0:256]
        wt[112 + 16 * dx : 128 + 16 * dx, 0:128] = block[:, 256:384]
    bias[...] = jnp.zeros_like(bias)
    bias[0:1, 0:384] = jnp.where(stem_ok, spread(b4[0:1], t384_f), 0.0)

    lane = iota((32, 256), 1)
    half, quarter = lane >> 7, (lane >> 5) & 3
    row_a = 2 + 2 * quarter + half
    ok_a = (quarter < 3) & within(y0 - 4 + row_a, full_y)
    row_a = jnp.where(ok_a, row_a, -99)
    xpar = quarter >> 1
    row_b = 8 * (quarter & 1) + half
    ok_b = within(y0 - 4 + row_b, full_y)
    row_b = jnp.where(ok_b, row_b, -99)
    reps = [dot_tn(w_skip[tap], t256) for tap in range(9)]
    for dx in range(3):
        for i in range(8):
            block = zero
            for a in range(3):
                block = jnp.where(row_a == 2 + i - a, reps[3 * a + dx], block)
            wa[256 * dx + 32 * i : 256 * dx + 32 * i + 32] = block.astype(BF16)
    for j in range(4):
        for i in range(8):
            t = ENDS[i]
            block = zero
            for a in range(3):
                for p in range(2):
                    if 0 <= j - p < 3:
                        block = jnp.where(
                            (row_b == t - a) & (xpar == p), reps[3 * a + j - p], block
                        )
            wb[256 * j + 32 * i : 256 * j + 32 * i + 32] = block.astype(BF16)
    b_skip = spread(b4[1:2], t256_f)
    bias[1:2, 0:256] = jnp.where(ok_a[0:1], b_skip, 0.0)
    bias[2:3, 0:256] = jnp.where(ok_b[0:1], b_skip, 0.0)

    slots = []
    for c in range(3):
        slots += [(1, c), (2, c), (3, c), ((None, 0), (0, 2), (4, 2))[c]]
    slots += [(0, 0), (4, 0), (0, 1), (4, 1)]
    q_of = lane >> 6
    for dx in range(3):
        reps = [dot_tn(w_coarse[3 * ca + dx], t64) for ca in range(9)]
        for i, (p, c) in enumerate(slots):
            block = zero
            if p is not None:
                for a in range(3):
                    block = jnp.where(q_of == p - a, reps[3 * c + a], block)
            wc[512 * dx + 32 * i : 512 * dx + 32 * i + 32] = block.astype(BF16)
    bias[3:4, 0:256] = spread(b_coarse[...], t64_f)

    lane64 = iota((64, 256), 1)
    quarter64 = (lane64 >> 5) & 3
    ok64 = within(y0 - 2 + 2 * quarter64 + (lane64 >> 7), full_y)
    rep = dot_tn(w_lift[...], t256)
    for q in range(3):
        wl[64 * q : 64 * q + 64] = jnp.where((quarter64 == q) & ok64, rep, 0.0).astype(BF16)
    wl[192:256] = jnp.zeros((64, 256), BF16)
    bias[4:5, 0:256] = jnp.where(ok_a[0:1], spread(b4[2:3], t256_f), 0.0)

    xi_of, f_of = lane >> 6, (lane >> 5) & 1
    reps = [dot_tn(w_final[tap], t256) for tap in range(9)]
    for j in range(6):
        for i in range(8):
            row = 2 + 2 * (i & 3) + (i >> 2)
            block = zero
            if (i & 3) < 3:
                for a in range(3):
                    for dx in range(3):
                        if 0 <= row - 3 - a < 2 and 0 <= j - dx < 4:
                            block = jnp.where(
                                (f_of == row - 3 - a) & (xi_of == j - dx), reps[3 * a + dx], block
                            )
            wf[256 * j + 32 * i : 256 * j + 32 * i + 32] = block.astype(BF16)
    bias[5:6, 0:256] = spread(b4[3:4], t256_f)

    row = iota((32, 256), 0)
    rep = dot(w_head[...], t256)
    block = zero
    for o in range(3):
        here = ((row >> 3) == xi_of) & ((row & 7) == 2 * o + f_of)
        block = jnp.where(here, rep[o : o + 1], block)
    wh[...] = block.astype(BF16)
    kind = iota((8, 512), 0)
    bias[8:16] = jnp.where(kind < 2, b_head[0], jnp.where(kind < 4, b_head[1], b_head[2]))
    for k, term in enumerate(in_three(bias[...])):
        wv[32 * k : 32 * k + 16] = term[:, 0:256]
        wv[32 * k + 16 : 32 * k + 32] = term[:, 256:512]


def prepare(pos, b_head, brick_y, full_y, w_stem, w_skip, w_coarse, w_lift, w_final, w_head, b4, b_coarse):
    vmem = pl.BlockSpec(memory_space=pltpu.VMEM)
    return pl.pallas_call(
        functools.partial(prep_kernel, brick_y, full_y),
        out_shape=jax.ShapeDtypeStruct((WEIGHT_ROWS, 256), BF16),
        in_specs=[pl.BlockSpec(memory_space=pltpu.SMEM)] * 2 + [vmem] * 8,
        out_specs=vmem,
        scratch_shapes=[pltpu.VMEM((16, 512), F32)],
        cost_estimate=pl.CostEstimate(
            flops=100_000_000, bytes_accessed=4_000_000, transcendentals=0
        ),
        compiler_params=pltpu.CompilerParams(vmem_limit_bytes=12 * MIB),
    )(pos, b_head, w_stem, w_skip, w_coarse, w_lift, w_final, w_head, b4, b_coarse)


def brick_kernel(
    parts_gz,
    cols,
    steps,
    pos_ref,
    r_ref,
    packed,
    out_ref,
    bias,
    tmp,
    rin,
    stem,
    skip,
    pooled,
    fin,
):
    wa, wb, wc, wl, wf, wh, ws, wt, wv = parts_of(packed)
    terms = [
        jnp.concatenate([wv[32 * k : 32 * k + 16], wv[32 * k + 16 : 32 * k + 32]], axis=1)
        for k in range(3)
    ]
    bias[...] = terms[0].astype(F32) + (terms[1].astype(F32) + terms[2].astype(F32))
    nz, have = r_ref.shape[0:2]
    pitch = tmp.shape[0] // nz
    blocks = cols // 8 + 2
    step = 0 if steps == 1 else pl.program_id(0)
    leftmost = (pos_ref[0] == 0) & (step == 0)
    rightmost = (pos_ref[0] == parts_gz - 1) & (step == steps - 1)

    def row_of(z):
        return z % (nz // 8) * 8 + z // (nz // 8)

    for z in range(nz):
        tmp[z * pitch : z * pitch + have] = r_ref[z].astype(F32)
    for b in range(blocks):
        rows = [
            tmp[pl.ds(step * (cols // 8) + b + k * pitch, 8, stride=nz // 8 * pitch), :]
            for k in range(nz // 8)
        ]
        rin[b] = jnp.concatenate(rows, axis=0).astype(BF16)

    b_stem = bias[0:1, 0:384]

    def stem_put(acc, first, i):
        out = relu(acc + b_stem).astype(BF16)
        low = iota((acc.shape[0], LANES), 1) < 64
        ends = jnp.where(low, out[:, 0:128], out[:, 128:256])
        for b in range(acc.shape[0] // nz):
            at = 4 * (first + b) + (i >> 1)
            stem[at, i & 1, :, 0:384] = out[b * nz : b * nz + nz]
            stem[at, i & 1, :, 384:512] = ends[b * nz : b * nz + nz]

    def weight_at(start, depth):
        return jnp.concatenate([ws[pl.ds(start, depth)], wt[pl.ds(start, depth), 0:128]], axis=1)

    def stem_mid(i, carry):
        start = pl.multiple_of(128 - 16 * i, 16)
        stem_put(dot(rin[...].reshape(blocks * nz, LANES), weight_at(start, LANES)), 0, i)
        return carry

    lax.fori_loop(1, 7, stem_mid, 0)
    pair = jnp.concatenate([rin[0 : blocks - 1], rin[1:blocks]], axis=-1)
    pair = pair.reshape((blocks - 1) * nz, 2 * LANES)
    stem_put(dot(pair, weight_at(0, 256)), 1, 0)
    stem_put(dot(pair, weight_at(16, 256)), 0, 7)

    @pl.when(leftmost)
    def _():
        stem[0:4] = jnp.zeros((4,) + stem.shape[1:], BF16)

    @pl.when(rightmost)
    def _():
        stem[4 * blocks - 4 : 4 * blocks] = jnp.zeros((4,) + stem.shape[1:], BF16)

    pairs = cols // 2 + 4
    mc = divisor(pairs, 1056 // nz)
    m_rows = mc * nz

    def skip_step(i, carry):
        m0 = i * mc

        def taken(u, half):
            part = stem[pl.ds(m0 + u // 2, mc), u % 2, :, 256 * half : 256 * half + 256]
            return part.reshape(m_rows, 256)

        near = [
            jnp.concatenate([taken(3 + k, 0), taken(4 + k, 0)], axis=0) for k in range(3)
        ]
        acc = dot(jnp.concatenate(near, axis=1), wa[...])
        acc = relu(acc + bias[1:2, 0:256])
        best = jnp.maximum(acc[:, 0:128], acc[:, 128:256])
        top = jnp.maximum(best[0:m_rows], best[m_rows:])
        for p in range(2):
            out = acc[p * m_rows : p * m_rows + m_rows].astype(BF16)
            skip[pl.ds(m0, mc), p] = out.reshape(mc, nz, 256)
        acc = dot(taken(3, 1), wb[0:256])
        for j in range(1, 4):
            acc += dot(taken(3 + j, 1), wb[256 * j : 256 * j + 256])
        best = jnp.maximum(acc[:, 0:128], acc[:, 128:256])
        best = jnp.maximum(best, pltpu.roll(best, 64, axis=1))
        ends = relu(best + bias[2:3, 0:128])
        lane = iota((m_rows, LANES), 1)
        sub = iota((mc, 1, 8, LANES), 2)

        def below(x):
            x = x.reshape(mc, nz // 8, 8, LANES)
            turned = jnp.where(sub == 0, 0.0, pltpu.roll(x[:, -1:], 1, axis=2))
            return jnp.concatenate([turned, x[:, :-1]], axis=1).reshape(m_rows, LANES)

        def above(x):
            x = x.reshape(mc, nz // 8, 8, LANES)
            turned = jnp.where(sub == 7, 0.0, pltpu.roll(x[:, :1], 7, axis=2))
            return jnp.concatenate([x[:, 1:], turned], axis=1).reshape(m_rows, LANES)

        ends_above = above(ends)
        parts = (
            below(top),
            jnp.where(lane < 96, top, pltpu.roll(ends_above, 32, axis=1)),
            jnp.where(lane < 96, above(top), ends_above),
            jnp.where(lane < 64, below(ends), ends),
        )
        for k in range(4):
            pooled[pl.ds(m0, mc), :, 128 * k : 128 * k + 128] = (
                parts[k].astype(BF16).reshape(mc, nz, LANES)
            )
        return carry

    lax.fori_loop(0, pairs // mc, skip_step, 0)

    @pl.when(leftmost)
    def _():
        pooled[0:2] = jnp.zeros((2,) + pooled.shape[1:], BF16)

    @pl.when(rightmost)
    def _():
        pooled[pairs - 2 : pairs] = jnp.zeros((2,) + pooled.shape[1:], BF16)

    count = cols // 2 + 2
    nc = divisor(count, 832 // nz)
    n_rows = nc * nz

    def coarse_step(i, carry):
        n0 = i * nc
        acc = dot(pooled[pl.ds(n0, nc)].reshape(n_rows, 512), wc[0:512])
        acc += dot(pooled[pl.ds(n0 + 1, nc)].reshape(n_rows, 512), wc[512:1024])
        acc += dot(pooled[pl.ds(n0 + 2, nc)].reshape(n_rows, 512), wc[1024:1536])
        coarse = relu(acc + bias[3:4, 0:256]).astype(BF16)
        lifted = dot(coarse, wl[...])
        for p in range(2):
            base = skip[pl.ds(n0 + 1, nc), p].reshape(n_rows, 256).astype(F32)
            out = relu(base + lifted + bias[4:5, 0:256]).astype(BF16)
            for k in range(nc):
                n = n0 + k
                stem[n >> 1, n & 1, :, 256 * p : 256 * p + 256] = out[k * nz : k * nz + nz]
        return carry

    lax.fori_loop(0, count // nc, coarse_step, 0)

    @pl.when(leftmost)
    def _():
        stem[0, 0] = jnp.zeros(stem.shape[2:], BF16)

    @pl.when(rightmost)
    def _():
        stem[cols // 4, 1] = jnp.zeros(stem.shape[2:], BF16)

    quads = cols // 4
    qc = divisor(quads, 1024 // nz)
    q_rows = qc * nz

    def final_step(i, carry):
        q0 = i * qc
        acc = jnp.zeros((q_rows, 256), F32)
        for j in range(6):
            k = (1 + j) % 4
            half = 256 * (k % 2)
            part = stem[pl.ds(q0 + (1 + j) // 4, qc), k // 2, :, half : half + 256]
            acc += dot(part.reshape(q_rows, 256), wf[256 * j : 256 * j + 256])
        out = relu(acc + bias[5:6, 0:256])
        for k in range(2):
            fin[k, pl.ds(pl.multiple_of(q0 * nz, 8), q_rows), :] = out[:, 128 * k : 128 * k + 128]
        return carry

    lax.fori_loop(0, quads // qc, final_step, 0)

    together = LANES // quads
    groups = nz // together
    lines = []
    for g in range(groups):
        sides = []
        for side in range(2):
            rows = [
                fin[side, pl.ds(row_of(g * together + k), quads, stride=nz), :]
                for k in range(together)
            ]
            sides.append(jnp.concatenate(rows, axis=0).astype(BF16))
        h = dot_nt(wh[...], jnp.concatenate(sides, axis=1))
        lines.append(jnp.concatenate([h[8 * xi : 8 * xi + 8] for xi in range(4)], axis=1))
    table = jnp.concatenate(lines, axis=0)
    size = together * cols
    row = iota((512, size), 0)
    order = jnp.where(iota((512, size), 1) == 4 * (row & 127) + (row >> 7), 1.0, 0.0).astype(BF16)
    high, middle, low = in_three(table)
    result = dot(high, order) + (dot(middle, order) + dot(low, order))
    result = result.reshape(groups, 8, size) + bias[8:16, 0:size]
    for g in range(groups):
        for k in range(together):
            for o in range(3):
                out_ref[o, g * together + k] = (
                    result[g, 2 * o : 2 * o + 2, k * cols : k * cols + cols]
                )


def brick(pos, received, weights, parts_gz, brick_y, brick_x):
    nz, have = received.shape[0:2]
    cols = brick_x
    while cols * nz > 16384 and cols % 256 == 0:
        cols //= 2
    steps = brick_x // cols
    scratch = [
        ((16, 512), F32),
        ((nz * round_up(have, 8), LANES), F32),
        ((cols // 8 + 2, nz, LANES), BF16),
        ((cols // 2 + 8, 2, nz, 512), BF16),
        ((cols // 2 + 4, 2, nz, 256), BF16),
        ((cols // 2 + 4, nz, 512), BF16),
        ((2, cols // 4 * nz, LANES), F32),
    ]
    operands = [(received.shape, BF16), (weights.shape, BF16), ((6, nz, 8, cols), F32)]
    held = sum(math.prod(shape) * jnp.dtype(dtype).itemsize for shape, dtype in scratch + operands)
    vmem = pl.BlockSpec(memory_space=pltpu.VMEM)
    smem = pl.BlockSpec(memory_space=pltpu.SMEM)
    return pl.pallas_call(
        functools.partial(brick_kernel, parts_gz, cols, steps),
        grid=(steps,),
        out_shape=jax.ShapeDtypeStruct((3, nz, brick_y, brick_x), F32),
        in_specs=[smem, vmem, vmem],
        out_specs=pl.BlockSpec((3, nz, brick_y, cols), lambda i: (0, 0, 0, i)),
        scratch_shapes=[pltpu.VMEM(shape, dtype) for shape, dtype in scratch],
        cost_estimate=pl.CostEstimate(
            flops=20_000_000_000, bytes_accessed=4_000_000, transcendentals=0
        ),
        compiler_params=pltpu.CompilerParams(vmem_limit_bytes=min(held + 6 * MIB, 60 * MIB)),
    )(pos, received, weights)


def local(
    image,
    offsets,
    w_stem,
    b_stem,
    w_skip,
    b_skip,
    w_coarse,
    b_coarse,
    w_lift,
    b_lift,
    w_final,
    b_final,
    w_head,
    b_head,
):
    parts_gz, parts_gy = lax.axis_size("gz"), lax.axis_size("gy")
    full_y, full_x = image.shape[1:]
    brick_y, brick_x = full_y // parts_gy, full_x // parts_gz
    assert image.shape[0] == 1 and brick_y == 2
    pos = jnp.stack([lax.axis_index("gz"), lax.axis_index("gy")]).astype(I32)
    windows = make_windows(image, offsets, parts_gz, parts_gy)
    received = lax.all_to_all(windows, ("gz", "gy"), 0, 0, tiled=True)
    b4 = jnp.stack([b_stem, b_skip, b_lift, b_final])
    weights = prepare(
        pos,
        b_head,
        brick_y,
        full_y,
        w_stem.reshape(w_stem.shape[0:2]),
        w_skip,
        w_coarse,
        w_lift,
        w_final,
        w_head,
        b4,
        b_coarse[None],
    )
    return brick(pos, received, weights, parts_gz, brick_y, brick_x)


def solution(mesh):
    split = P(("gz", "gy"))
    return jax.shard_map(
        local,
        mesh=mesh,
        in_specs=(split, split) + (P(),) * 12,
        out_specs=P(None, None, "gy", "gz"),
        check_vma=False,
    )
```

```python
import functools
import math

import jax
import jax.numpy as jnp
from jax import lax
from jax.experimental import pallas as pl
from jax.experimental.pallas import tpu as pltpu
from jax.sharding import PartitionSpec as P

MAXOFF = 32
LANES = 128
PAD = MAXOFF + 8
BF16, F32, I32 = jnp.bfloat16, jnp.float32, jnp.int32
MIB = 1024 * 1024


def packing(brick_x, nz):
    return (9, 14, 6, 6) if chunk(brick_x, nz) == brick_x else (8, 16, 8, 7)


def chunk(brick_x, nz):
    cols = brick_x
    while cols * nz > 16384 and cols % 256 == 0:
        cols //= 2
    return cols


def iota(shape, dim):
    return lax.broadcasted_iota(I32, shape, dim)


def dot(a, b):
    return jnp.dot(a, b, preferred_element_type=F32)


def dot_tn(a, b):
    return lax.dot_general(a, b, (((0,), (0,)), ((), ())), preferred_element_type=F32)


def dot_nt(a, b):
    return lax.dot_general(a, b, (((1,), (1,)), ((), ())), preferred_element_type=F32)


def relu(x):
    return jnp.maximum(x, 0.0)


def round_up(n, m):
    return -(-n // m) * m


def divisor(count, most):
    return max(d for d in range(1, count + 1) if count % d == 0 and d <= max(most, 1))


def send_kernel(parts_gz, parts_gy, brick_y, brick_x, pack, off_ref, image_ref, send_ref, tall_ref):
    count, slots, ahead_x, ahead_y = pack
    full_y, full_x = image_ref.shape[1:]
    rows = send_ref.shape[1]
    off_y, off_x = off_ref[0, 0], off_ref[0, 1]
    tall_ref[...] = jnp.zeros_like(tall_ref)
    tall_ref[PAD : PAD + full_x, 0:full_y] = image_ref[0].astype(F32).T
    lane = iota((rows, LANES), 1)
    slot = lane
    for i in range(1, count):
        slot = jnp.where(lane >= slots * i, lane - slots * i, slot)
    block = iota((rows, LANES), 0) * count
    parts = -(-full_y // slots)
    for gz in range(parts_gz):
        packed = [jnp.zeros((rows, LANES), F32) for _ in range(parts)]
        for i in range(count):
            x = gz * brick_x - ahead_x + i
            column = tall_ref[pl.ds(PAD + x - off_x, rows, stride=count), :]
            here = (lane >= slots * i) & (lane < slots * i + slots)
            here &= (block >= -x) & (block < full_x - x)
            for h in range(parts):
                turn = lax.rem(off_y + (slots * (i - h) + 2 * LANES), LANES)
                turned = pltpu.roll(column, turn, axis=1)
                packed[h] = jnp.where(here & (slot < full_y - slots * h), turned, packed[h])
        for gy in range(parts_gy):
            window = jnp.zeros((rows, LANES), F32)
            for h in range(parts):
                shift = brick_y * gy - ahead_y - slots * h
                if -slots < shift < slots:
                    turned = packed[h]
                    if shift:
                        turned = pltpu.roll(turned, (-shift) % LANES, axis=1)
                    inside = (slot + shift >= 0) & (slot + shift < slots)
                    window = jnp.where(inside, turned, window)
            send_ref[gz * parts_gy + gy] = window.astype(BF16)


def make_windows(image, offsets, parts_gz, parts_gy, nz):
    full_y, full_x = image.shape[1:]
    brick_y, brick_x = full_y // parts_gy, full_x // parts_gz
    pack = packing(brick_x, nz)
    rows = round_up(-(-(brick_x + 6 + pack[2]) // pack[0]), 8)
    tall = round_up(PAD + full_x - brick_x + MAXOFF + pack[0] * rows, 8)
    return pl.pallas_call(
        functools.partial(send_kernel, parts_gz, parts_gy, brick_y, brick_x, pack),
        out_shape=jax.ShapeDtypeStruct((parts_gz * parts_gy, rows, LANES), BF16),
        in_specs=[
            pl.BlockSpec(memory_space=pltpu.SMEM),
            pl.BlockSpec(memory_space=pltpu.VMEM),
        ],
        out_specs=pl.BlockSpec(memory_space=pltpu.VMEM),
        scratch_shapes=[pltpu.VMEM((tall, LANES), F32)],
    )(offsets, image)


ENDS = (0, 1, 10, 11, 2, 3, 8, 9)


SIZES = {"a": 768, "b": 1024, "c": 1536, "l": 256, "f": 1536, "h": 32, "v": 96, "s": 736, "t": 368}
STARTS = dict(zip(SIZES, [sum(list(SIZES.values())[:k]) for k in range(len(SIZES))]))
MIDDLE = 96
WEIGHT_ROWS = sum(SIZES.values())


def parts_of(ref):
    return [ref.at[STARTS[k] : STARTS[k] + SIZES[k]] for k in SIZES]


def in_three(x):
    high = x.astype(BF16)
    rest = x - high.astype(F32)
    middle = rest.astype(BF16)
    return high, middle, (rest - middle.astype(F32)).astype(BF16)


def stem_row(s):
    return jnp.where(s < 8, s + 2, jnp.where(s < 10, s - 8, s))


def within(y, full_y):
    return (y >= 0) & (y < full_y)


def prep_kernel(
    brick_y,
    full_y,
    pack,
    pos_ref,
    b_head,
    w_stem,
    w_skip,
    w_coarse,
    w_lift,
    w_final,
    w_head,
    b4,
    b_coarse,
    packed,
    bias,
):
    wa, wb, wc, wl, wf, wh, wv, ws, wt = parts_of(packed)
    y0 = pos_ref[1] * brick_y
    zero = jnp.zeros((32, 256), F32)

    def tiles(count, width):
        return jnp.where((iota((count, width), 1) & (count - 1)) == iota((count, width), 0), 1.0, 0.0)

    t384_f, t256_f, t64_f = tiles(32, 384), tiles(32, 256), tiles(64, 256)
    t384, t256, t64 = t384_f.astype(BF16), t256_f.astype(BF16), t64_f.astype(BF16)

    def spread(row, table):
        return jnp.dot(row, table, precision=lax.Precision.HIGHEST, preferred_element_type=F32)

    lane = iota((1, 384), 1)
    t_of = stem_row(lane >> 5)
    stem_ok = within(y0 - 5 + t_of, full_y)
    rep = dot(w_stem[...], t384)
    lane16 = iota((16, 384), 1)
    t16 = stem_row(lane16 >> 5)
    tap16 = iota((16, 384), 0) - t16
    ok16 = within(y0 - 5 + t16, full_y)
    taps = []
    for dx in range(3):
        block = jnp.zeros((16, 384), F32)
        for a in range(3):
            block = jnp.where((tap16 == a) & ok16, rep[3 * a + dx : 3 * a + dx + 1], block)
        taps.append(block)
    taps = jnp.concatenate(taps, axis=0).astype(BF16)
    count, slots, _, ahead_y = pack
    for part, i in enumerate((0, count - 1, None)):
        depth = 256 if part < 2 else 224
        row, column = iota((depth, 48), 0), iota((depth, 48), 1)
        place = jnp.zeros((depth, 48), F32)
        for dx in range(3):
            if part < 2:
                at = i - 1 + dx
                start = slots * (at % count) + 128 * (at // count + (i == 0))
            else:
                start = MIDDLE + slots * dx
            near = (column >= 16 * dx) & (column < 16 * dx + 14)
            here = row == start + ahead_y - 6 + column - 16 * dx
            place = jnp.where(near & here, 1.0, place)
        block = dot(place.astype(BF16), taps).astype(BF16)
        ws[256 * part : 256 * part + depth] = block[:, 0:256]
        if part < 2:
            wt[0:256, 128 * part : 128 * part + 128] = block[:, 256:384]
        else:
            wt[256:368, 0:128] = block[0:112, 256:384]
            wt[256:368, 128:256] = block[112:224, 256:384]
    bias[...] = jnp.zeros_like(bias)
    bias[0:1, 0:384] = jnp.where(stem_ok, spread(b4[0:1], t384_f), 0.0)

    lane = iota((32, 256), 1)
    half, quarter = lane >> 7, (lane >> 5) & 3
    row_a = 2 + 2 * quarter + half
    ok_a = (quarter < 3) & within(y0 - 4 + row_a, full_y)
    row_a = jnp.where(ok_a, row_a, -99)
    xpar = quarter >> 1
    row_b = 8 * (quarter & 1) + half
    ok_b = within(y0 - 4 + row_b, full_y)
    row_b = jnp.where(ok_b, row_b, -99)
    reps = [dot_tn(w_skip[tap], t256) for tap in range(9)]
    for dx in range(3):
        for i in range(8):
            block = zero
            for a in range(3):
                block = jnp.where(row_a == 2 + i - a, reps[3 * a + dx], block)
            wa[256 * dx + 32 * i : 256 * dx + 32 * i + 32] = block.astype(BF16)
    for j in range(4):
        for i in range(8):
            t = ENDS[i]
            block = zero
            for a in range(3):
                for p in range(2):
                    if 0 <= j - p < 3:
                        block = jnp.where(
                            (row_b == t - a) & (xpar == p), reps[3 * a + j - p], block
                        )
            wb[256 * j + 32 * i : 256 * j + 32 * i + 32] = block.astype(BF16)
    b_skip = spread(b4[1:2], t256_f)
    bias[1:2, 0:256] = jnp.where(ok_a[0:1], b_skip, 0.0)
    bias[2:3, 0:256] = jnp.where(ok_b[0:1], b_skip, 0.0)

    slots = []
    for c in range(3):
        slots += [(1, c), (2, c), (3, c), ((None, 0), (0, 2), (4, 2))[c]]
    slots += [(0, 0), (4, 0), (0, 1), (4, 1)]
    q_of = lane >> 6
    for dx in range(3):
        reps = [dot(w_coarse[3 * ca + dx], t64) for ca in range(9)]
        for i, (p, c) in enumerate(slots):
            block = zero
            if p is not None:
                for a in range(3):
                    block = jnp.where(q_of == p - a, reps[3 * c + a], block)
            wc[512 * dx + 32 * i : 512 * dx + 32 * i + 32] = block.astype(BF16)
    bias[3:4, 0:256] = spread(b_coarse[...], t64_f)

    lane64 = iota((64, 256), 1)
    quarter64 = (lane64 >> 5) & 3
    ok64 = within(y0 - 2 + 2 * quarter64 + (lane64 >> 7), full_y)
    rep = dot_tn(w_lift[...], t256)
    for q in range(3):
        wl[64 * q : 64 * q + 64] = jnp.where((quarter64 == q) & ok64, rep, 0.0).astype(BF16)
    wl[192:256] = jnp.zeros((64, 256), BF16)
    bias[4:5, 0:256] = jnp.where(ok_a[0:1], spread(b4[2:3], t256_f), 0.0)

    xi_of, f_of = lane >> 6, (lane >> 5) & 1
    reps = [dot_tn(w_final[tap], t256) for tap in range(9)]
    for j in range(6):
        for i in range(8):
            row = 2 + 2 * (i & 3) + (i >> 2)
            block = zero
            if (i & 3) < 3:
                for a in range(3):
                    for dx in range(3):
                        if 0 <= row - 3 - a < 2 and 0 <= j - dx < 4:
                            block = jnp.where(
                                (f_of == row - 3 - a) & (xi_of == j - dx), reps[3 * a + dx], block
                            )
            wf[256 * j + 32 * i : 256 * j + 32 * i + 32] = block.astype(BF16)
    bias[5:6, 0:256] = spread(b4[3:4], t256_f)

    row = iota((32, 256), 0)
    rep = dot(w_head[...], t256)
    block = zero
    for o in range(3):
        here = ((row >> 3) == xi_of) & ((row & 7) == 2 * o + f_of)
        block = jnp.where(here, rep[o : o + 1], block)
    wh[...] = block.astype(BF16)
    kind = iota((8, 512), 0)
    bias[8:16] = jnp.where(kind < 2, b_head[0], jnp.where(kind < 4, b_head[1], b_head[2]))
    for k, term in enumerate(in_three(bias[...])):
        wv[32 * k : 32 * k + 16] = term[:, 0:256]
        wv[32 * k + 16 : 32 * k + 32] = term[:, 256:512]


def prepare(pos, b_head, brick_y, full_y, pack, w_stem, w_skip, w_coarse, w_lift, w_final, w_head, b4, b_coarse):
    vmem = pl.BlockSpec(memory_space=pltpu.VMEM)
    return pl.pallas_call(
        functools.partial(prep_kernel, brick_y, full_y, pack),
        out_shape=jax.ShapeDtypeStruct((WEIGHT_ROWS, 256), BF16),
        in_specs=[pl.BlockSpec(memory_space=pltpu.SMEM)] * 2 + [vmem] * 8,
        out_specs=vmem,
        scratch_shapes=[pltpu.VMEM((16, 512), F32)],
        cost_estimate=pl.CostEstimate(
            flops=100_000_000, bytes_accessed=4_000_000, transcendentals=0
        ),
        compiler_params=pltpu.CompilerParams(vmem_limit_bytes=12 * MIB),
    )(pos, b_head, w_stem, w_skip, w_coarse, w_lift, w_final, w_head, b4, b_coarse)


def brick_kernel(
    parts_gz,
    cols,
    steps,
    pack,
    pos_ref,
    r_ref,
    packed,
    out_ref,
    bias,
    shared,
    middle,
    tmp,
    rin,
    stem,
    skip,
    pooled,
    fin,
):
    wa, wb, wc, wl, wf, wh, wv, ws, wt = parts_of(packed)
    terms = [
        jnp.concatenate([wv[32 * k : 32 * k + 16], wv[32 * k + 16 : 32 * k + 32]], axis=1)
        for k in range(3)
    ]
    bias[...] = terms[0].astype(F32) + (terms[1].astype(F32) + terms[2].astype(F32))
    nz, have = r_ref.shape[0:2]
    pitch = tmp.shape[0] // nz
    per, slots, ahead_x, _ = pack
    blocks = -(-(cols + 6 + ahead_x) // per)
    step = 0 if steps == 1 else pl.program_id(0)
    leftmost = (pos_ref[0] == 0) & (step == 0)
    rightmost = (pos_ref[0] == parts_gz - 1) & (step == steps - 1)

    def row_of(z):
        return z % (nz // 8) * 8 + z // (nz // 8)

    for z in range(nz):
        tmp[z * pitch : z * pitch + have] = r_ref[z].astype(F32)
    for b in range(blocks):
        rows = [
            tmp[pl.ds(step * (cols // 8) + b + k * pitch, 8, stride=nz // 8 * pitch), :]
            for k in range(nz // 8)
        ]
        rin[b] = jnp.concatenate(rows, axis=0).astype(BF16)

    b_stem = bias[0:1, 0:384]

    def stem_put(acc, first, i):
        out = relu(acc + b_stem).astype(BF16)
        low = iota((acc.shape[0], LANES), 1) < 64
        ends = jnp.where(low, out[:, 0:128], out[:, 128:256])
        for b in range(acc.shape[0] // nz):
            u = per * (first + b) + i + 8 - ahead_x
            stem[u >> 1, u & 1, :, 0:384] = out[b * nz : b * nz + nz]
            stem[u >> 1, u & 1, :, 384:512] = ends[b * nz : b * nz + nz]

    shared[:, 0:256] = ws[512:736].astype(F32)
    shared[0:112, 256:384] = wt[256:368, 0:128].astype(F32)
    shared[112:224, 256:384] = wt[256:368, 128:256].astype(F32)

    for i in range(per - 2):
        start = MIDDLE - slots * i
        middle[i] = shared[start : start + LANES, :].astype(BF16)

    def stem_mid(i, carry):
        stem_put(dot(rin[...].reshape(blocks * nz, LANES), middle[i - 1]), 0, i)
        return carry

    lax.fori_loop(1, per - 1, stem_mid, 0)
    pair = jnp.concatenate([rin[0 : blocks - 1], rin[1:blocks]], axis=-1)
    pair = pair.reshape((blocks - 1) * nz, 2 * LANES)
    for part, (first, i) in enumerate(((1, 0), (0, per - 1))):
        weight = jnp.concatenate(
            [ws[256 * part : 256 * part + 256], wt[0:256, 128 * part : 128 * part + 128]], axis=1
        )
        stem_put(dot(pair, weight), first, i)

    @pl.when(leftmost)
    def _():
        stem[0:4] = jnp.zeros((4,) + stem.shape[1:], BF16)

    @pl.when(rightmost)
    def _():
        stem[cols // 2 + 4 : cols // 2 + 8] = jnp.zeros((4,) + stem.shape[1:], BF16)

    pairs = cols // 2 + 4
    mc = divisor(pairs, 1056 // nz)
    m_rows = mc * nz

    def skip_step(i, carry):
        m0 = i * mc

        def taken(u, half):
            part = stem[pl.ds(m0 + u // 2, mc), u % 2, :, 256 * half : 256 * half + 256]
            return part.reshape(m_rows, 256)

        near = [
            jnp.concatenate([taken(3 + k, 0), taken(4 + k, 0)], axis=0) for k in range(3)
        ]
        acc = dot(jnp.concatenate(near, axis=1), wa[...])
        acc = relu(acc + bias[1:2, 0:256])
        best = jnp.maximum(acc[:, 0:128], acc[:, 128:256])
        top = jnp.maximum(best[0:m_rows], best[m_rows:])
        for p in range(2):
            out = acc[p * m_rows : p * m_rows + m_rows].astype(BF16)
            skip[pl.ds(m0, mc), p] = out.reshape(mc, nz, 256)
        acc = dot(taken(3, 1), wb[0:256])
        for j in range(1, 4):
            acc += dot(taken(3 + j, 1), wb[256 * j : 256 * j + 256])
        best = jnp.maximum(acc[:, 0:128], acc[:, 128:256])
        best = jnp.maximum(best, pltpu.roll(best, 64, axis=1))
        ends = relu(best + bias[2:3, 0:128])
        lane = iota((m_rows, LANES), 1)
        sub = iota((mc, 1, 8, LANES), 2)

        def below(x):
            x = x.reshape(mc, nz // 8, 8, LANES)
            turned = jnp.where(sub == 0, 0.0, pltpu.roll(x[:, -1:], 1, axis=2))
            return jnp.concatenate([turned, x[:, :-1]], axis=1).reshape(m_rows, LANES)

        def above(x):
            x = x.reshape(mc, nz // 8, 8, LANES)
            turned = jnp.where(sub == 7, 0.0, pltpu.roll(x[:, :1], 7, axis=2))
            return jnp.concatenate([x[:, 1:], turned], axis=1).reshape(m_rows, LANES)

        ends_above = above(ends)
        parts = (
            below(top),
            jnp.where(lane < 96, top, pltpu.roll(ends_above, 32, axis=1)),
            jnp.where(lane < 96, above(top), ends_above),
            jnp.where(lane < 64, below(ends), ends),
        )
        for k in range(4):
            pooled[pl.ds(m0, mc), :, 128 * k : 128 * k + 128] = (
                parts[k].astype(BF16).reshape(mc, nz, LANES)
            )
        return carry

    lax.fori_loop(0, pairs // mc, skip_step, 0)

    @pl.when(leftmost)
    def _():
        pooled[0:2] = jnp.zeros((2,) + pooled.shape[1:], BF16)

    @pl.when(rightmost)
    def _():
        pooled[pairs - 2 : pairs] = jnp.zeros((2,) + pooled.shape[1:], BF16)

    count = cols // 2 + 2
    nc = divisor(count, 832 // nz)
    n_rows = nc * nz

    def coarse_step(i, carry):
        n0 = i * nc
        acc = dot(pooled[pl.ds(n0, nc)].reshape(n_rows, 512), wc[0:512])
        acc += dot(pooled[pl.ds(n0 + 1, nc)].reshape(n_rows, 512), wc[512:1024])
        acc += dot(pooled[pl.ds(n0 + 2, nc)].reshape(n_rows, 512), wc[1024:1536])
        coarse = relu(acc + bias[3:4, 0:256]).astype(BF16)
        lifted = dot(coarse, wl[...])
        for p in range(2):
            base = skip[pl.ds(n0 + 1, nc), p].reshape(n_rows, 256).astype(F32)
            out = relu(base + lifted + bias[4:5, 0:256]).astype(BF16)
            for k in range(nc):
                n = n0 + k
                stem[n >> 1, n & 1, :, 256 * p : 256 * p + 256] = out[k * nz : k * nz + nz]
        return carry

    lax.fori_loop(0, count // nc, coarse_step, 0)

    @pl.when(leftmost)
    def _():
        stem[0, 0] = jnp.zeros(stem.shape[2:], BF16)

    @pl.when(rightmost)
    def _():
        stem[cols // 4, 1] = jnp.zeros(stem.shape[2:], BF16)

    quads = cols // 4
    qc = divisor(quads, 1024 // nz)
    q_rows = qc * nz

    def final_step(i, carry):
        q0 = i * qc
        acc = jnp.zeros((q_rows, 256), F32)
        for j in range(6):
            k = (1 + j) % 4
            half = 256 * (k % 2)
            part = stem[pl.ds(q0 + (1 + j) // 4, qc), k // 2, :, half : half + 256]
            acc += dot(part.reshape(q_rows, 256), wf[256 * j : 256 * j + 256])
        out = relu(acc + bias[5:6, 0:256])
        for k in range(2):
            fin[k, pl.ds(pl.multiple_of(q0 * nz, 8), q_rows), :] = out[:, 128 * k : 128 * k + 128]
        return carry

    lax.fori_loop(0, quads // qc, final_step, 0)

    together = LANES // quads
    groups = nz // together
    lines = []
    for g in range(groups):
        sides = []
        for side in range(2):
            rows = [
                fin[side, pl.ds(row_of(g * together + k), quads, stride=nz), :]
                for k in range(together)
            ]
            sides.append(jnp.concatenate(rows, axis=0).astype(BF16))
        h = dot_nt(wh[...], jnp.concatenate(sides, axis=1))
        lines.append(jnp.concatenate([h[8 * xi : 8 * xi + 8] for xi in range(4)], axis=1))
    table = jnp.concatenate(lines, axis=0)
    size = together * cols
    row = iota((512, size), 0)
    order = jnp.where(iota((512, size), 1) == 4 * (row & 127) + (row >> 7), 1.0, 0.0).astype(BF16)
    high, middle, low = in_three(table)
    result = dot(high, order) + (dot(middle, order) + dot(low, order))
    result = result.reshape(groups, 8, size) + bias[8:16, 0:size]
    for g in range(groups):
        for k in range(together):
            for o in range(3):
                out_ref[o, g * together + k] = (
                    result[g, 2 * o : 2 * o + 2, k * cols : k * cols + cols]
                )


def brick(pos, received, weights, parts_gz, brick_y, brick_x):
    nz, have = received.shape[0:2]
    cols, pack = chunk(brick_x, nz), packing(brick_x, nz)
    steps = brick_x // cols
    scratch = [
        ((16, 512), F32),
        ((224, 384), F32),
        ((pack[0] - 2, LANES, 384), BF16),
        ((nz * round_up(have, 8), LANES), F32),
        ((-(-(cols + 6 + pack[2]) // pack[0]), nz, LANES), BF16),
        ((cols // 2 + 8, 2, nz, 512), BF16),
        ((cols // 2 + 4, 2, nz, 256), BF16),
        ((cols // 2 + 4, nz, 512), BF16),
        ((2, cols // 4 * nz, LANES), F32),
    ]
    operands = [(received.shape, BF16), (weights.shape, BF16), ((6, nz, 8, cols), F32)]
    held = sum(math.prod(shape) * jnp.dtype(dtype).itemsize for shape, dtype in scratch + operands)
    vmem = pl.BlockSpec(memory_space=pltpu.VMEM)
    smem = pl.BlockSpec(memory_space=pltpu.SMEM)
    return pl.pallas_call(
        functools.partial(brick_kernel, parts_gz, cols, steps, pack),
        grid=(steps,),
        out_shape=jax.ShapeDtypeStruct((3, nz, brick_y, brick_x), F32),
        in_specs=[smem, vmem, vmem],
        out_specs=pl.BlockSpec((3, nz, brick_y, cols), lambda i: (0, 0, 0, i)),
        scratch_shapes=[pltpu.VMEM(shape, dtype) for shape, dtype in scratch],
        cost_estimate=pl.CostEstimate(
            flops=20_000_000_000, bytes_accessed=4_000_000, transcendentals=0
        ),
        compiler_params=pltpu.CompilerParams(vmem_limit_bytes=min(held + 6 * MIB, 60 * MIB)),
    )(pos, received, weights)


def local(
    image,
    offsets,
    w_stem,
    b_stem,
    w_skip,
    b_skip,
    w_coarse,
    b_coarse,
    w_lift,
    b_lift,
    w_final,
    b_final,
    w_head,
    b_head,
):
    parts_gz, parts_gy = lax.axis_size("gz"), lax.axis_size("gy")
    full_y, full_x = image.shape[1:]
    brick_y, brick_x = full_y // parts_gy, full_x // parts_gz
    assert image.shape[0] == 1 and brick_y == 2
    pos = jnp.stack([lax.axis_index("gz"), lax.axis_index("gy")]).astype(I32)
    nz = parts_gz * parts_gy
    windows = make_windows(image, offsets, parts_gz, parts_gy, nz)
    received = lax.all_to_all(windows, ("gz", "gy"), 0, 0, tiled=True)
    b4 = jnp.stack([b_stem, b_skip, b_lift, b_final])
    weights = prepare(
        pos,
        b_head,
        brick_y,
        full_y,
        packing(brick_x, nz),
        w_stem.reshape(w_stem.shape[0:2]),
        w_skip,
        w_coarse.transpose(0, 2, 1),
        w_lift,
        w_final,
        w_head,
        b4,
        b_coarse[None],
    )
    return brick(pos, received, weights, parts_gz, brick_y, brick_x)


def solution(mesh):
    split = P(("gz", "gy"))
    return jax.shard_map(
        local,
        mesh=mesh,
        in_specs=(split, split) + (P(),) * 12,
        out_specs=P(None, None, "gy", "gz"),
        check_vma=False,
    )
```

```python
import functools
import math

import jax
import jax.numpy as jnp
from jax import lax
from jax.experimental import pallas as pl
from jax.experimental.pallas import tpu as pltpu
from jax.sharding import PartitionSpec as P

MAXOFF = 32
LANES = 128
PAD = MAXOFF + 8
BF16, F32, I32 = jnp.bfloat16, jnp.float32, jnp.int32
MIB = 1024 * 1024


def packing(brick_x, nz):
    return (9, 14, 6, 6) if chunk(brick_x, nz) == brick_x else (8, 16, 8, 7)


def chunk(brick_x, nz):
    cols = brick_x
    while cols * nz > 16384 and cols % 256 == 0:
        cols //= 2
    return cols


def iota(shape, dim):
    return lax.broadcasted_iota(I32, shape, dim)


def dot(a, b):
    return jnp.dot(a, b, preferred_element_type=F32)


def dot_tn(a, b):
    return lax.dot_general(a, b, (((0,), (0,)), ((), ())), preferred_element_type=F32)


def dot_nt(a, b):
    return lax.dot_general(a, b, (((1,), (1,)), ((), ())), preferred_element_type=F32)


def relu(x):
    return jnp.maximum(x, 0.0)


def round_up(n, m):
    return -(-n // m) * m


def divisor(count, most):
    return max(d for d in range(1, count + 1) if count % d == 0 and d <= max(most, 1))


def send_kernel(parts_gz, parts_gy, brick_y, brick_x, pack, off_ref, image_ref, send_ref, tall_ref):
    count, slots, ahead_x, ahead_y = pack
    full_y, full_x = image_ref.shape[1:]
    rows = send_ref.shape[1]
    off_y, off_x = off_ref[0, 0], off_ref[0, 1]
    tall_ref[...] = jnp.zeros_like(tall_ref)
    tall_ref[PAD : PAD + full_x, 0:full_y] = image_ref[0].astype(F32).T
    lane = iota((rows, LANES), 1)
    slot = lane
    for i in range(1, count):
        slot = jnp.where(lane >= slots * i, lane - slots * i, slot)
    block = iota((rows, LANES), 0) * count
    parts = -(-full_y // slots)
    for gz in range(parts_gz):
        packed = [jnp.zeros((rows, LANES), F32) for _ in range(parts)]
        for i in range(count):
            x = gz * brick_x - ahead_x + i
            column = tall_ref[pl.ds(PAD + x - off_x, rows, stride=count), :]
            here = (lane >= slots * i) & (lane < slots * i + slots)
            here &= (block >= -x) & (block < full_x - x)
            for h in range(parts):
                turn = lax.rem(off_y + (slots * (i - h) + 2 * LANES), LANES)
                turned = pltpu.roll(column, turn, axis=1)
                packed[h] = jnp.where(here & (slot < full_y - slots * h), turned, packed[h])
        for gy in range(parts_gy):
            window = jnp.zeros((rows, LANES), F32)
            for h in range(parts):
                shift = brick_y * gy - ahead_y - slots * h
                if -slots < shift < slots:
                    turned = packed[h]
                    if shift:
                        turned = pltpu.roll(turned, (-shift) % LANES, axis=1)
                    inside = (slot + shift >= 0) & (slot + shift < slots)
                    window = jnp.where(inside, turned, window)
            send_ref[gz * parts_gy + gy] = window.astype(BF16)


def make_windows(image, offsets, parts_gz, parts_gy, nz):
    full_y, full_x = image.shape[1:]
    brick_y, brick_x = full_y // parts_gy, full_x // parts_gz
    pack = packing(brick_x, nz)
    rows = round_up(-(-(brick_x + 6 + pack[2]) // pack[0]), 8)
    tall = round_up(PAD + full_x - brick_x + MAXOFF + pack[0] * rows, 8)
    return pl.pallas_call(
        functools.partial(send_kernel, parts_gz, parts_gy, brick_y, brick_x, pack),
        out_shape=jax.ShapeDtypeStruct((parts_gz * parts_gy, rows, LANES), BF16),
        in_specs=[
            pl.BlockSpec(memory_space=pltpu.SMEM),
            pl.BlockSpec(memory_space=pltpu.VMEM),
        ],
        out_specs=pl.BlockSpec(memory_space=pltpu.VMEM),
        scratch_shapes=[pltpu.VMEM((tall, LANES), F32)],
    )(offsets, image)


ENDS = (0, 1, 10, 11, 2, 3, 8, 9)


SIZES = {"a": 768, "b": 1024, "c": 1536, "l": 256, "f": 1536, "h": 32, "v": 96, "s": 736, "t": 368}
STARTS = dict(zip(SIZES, [sum(list(SIZES.values())[:k]) for k in range(len(SIZES))]))
MIDDLE = 96
WEIGHT_ROWS = sum(SIZES.values())


def parts_of(ref):
    return [ref.at[STARTS[k] : STARTS[k] + SIZES[k]] for k in SIZES]


def in_three(x):
    high = x.astype(BF16)
    rest = x - high.astype(F32)
    middle = rest.astype(BF16)
    return high, middle, (rest - middle.astype(F32)).astype(BF16)


def stem_row(s):
    return jnp.where(s < 8, s + 2, jnp.where(s < 10, s - 8, s))


def within(y, full_y):
    return (y >= 0) & (y < full_y)


def prep_kernel(
    brick_y,
    full_y,
    pack,
    pos_ref,
    b_head,
    w_stem,
    w_skip,
    w_coarse,
    w_lift,
    w_final,
    w_head,
    b4,
    b_coarse,
    packed,
    bias,
):
    wa, wb, wc, wl, wf, wh, wv, ws, wt = parts_of(packed)
    y0 = pos_ref[1] * brick_y
    zero = jnp.zeros((32, 256), F32)

    def tiles(count, width):
        return jnp.where((iota((count, width), 1) & (count - 1)) == iota((count, width), 0), 1.0, 0.0)

    t384_f, t256_f, t64_f = tiles(32, 384), tiles(32, 256), tiles(64, 256)
    t384, t256, t64 = t384_f.astype(BF16), t256_f.astype(BF16), t64_f.astype(BF16)

    def spread(row, table):
        return jnp.dot(row, table, precision=lax.Precision.HIGHEST, preferred_element_type=F32)

    lane = iota((1, 384), 1)
    t_of = stem_row(lane >> 5)
    stem_ok = within(y0 - 5 + t_of, full_y)
    rep = dot(w_stem[...], t384)
    lane16 = iota((16, 384), 1)
    t16 = stem_row(lane16 >> 5)
    tap16 = iota((16, 384), 0) - t16
    ok16 = within(y0 - 5 + t16, full_y)
    taps = []
    for dx in range(3):
        block = jnp.zeros((16, 384), F32)
        for a in range(3):
            block = jnp.where((tap16 == a) & ok16, rep[3 * a + dx : 3 * a + dx + 1], block)
        taps.append(block)
    taps = jnp.concatenate(taps, axis=0).astype(BF16)
    count, slots, _, ahead_y = pack
    for part, i in enumerate((0, count - 1, None)):
        depth = 256 if part < 2 else 224
        row, column = iota((depth, 48), 0), iota((depth, 48), 1)
        place = jnp.zeros((depth, 48), F32)
        for dx in range(3):
            if part < 2:
                at = i - 1 + dx
                start = slots * (at % count) + 128 * (at // count + (i == 0))
            else:
                start = MIDDLE + slots * dx
            near = (column >= 16 * dx) & (column < 16 * dx + 14)
            here = row == start + ahead_y - 6 + column - 16 * dx
            place = jnp.where(near & here, 1.0, place)
        block = dot(place.astype(BF16), taps).astype(BF16)
        ws[256 * part : 256 * part + depth] = block[:, 0:256]
        if part < 2:
            wt[0:256, 128 * part : 128 * part + 128] = block[:, 256:384]
        else:
            wt[256:368, 0:128] = block[0:112, 256:384]
            wt[256:368, 128:256] = block[112:224, 256:384]
    bias[...] = jnp.zeros_like(bias)
    bias[0:1, 0:384] = jnp.where(stem_ok, spread(b4[0:1], t384_f), 0.0)

    lane = iota((32, 256), 1)
    half, quarter = lane >> 7, (lane >> 5) & 3
    row_a = 2 + 2 * quarter + half
    ok_a = (quarter < 3) & within(y0 - 4 + row_a, full_y)
    row_a = jnp.where(ok_a, row_a, -99)
    xpar = quarter >> 1
    row_b = 8 * (quarter & 1) + half
    ok_b = within(y0 - 4 + row_b, full_y)
    row_b = jnp.where(ok_b, row_b, -99)
    reps = [dot_tn(w_skip[tap], t256) for tap in range(9)]
    for dx in range(3):
        for i in range(8):
            block = zero
            for a in range(3):
                block = jnp.where(row_a == 2 + i - a, reps[3 * a + dx], block)
            wa[256 * dx + 32 * i : 256 * dx + 32 * i + 32] = block.astype(BF16)
    for j in range(4):
        for i in range(8):
            t = ENDS[i]
            block = zero
            for a in range(3):
                for p in range(2):
                    if 0 <= j - p < 3:
                        block = jnp.where(
                            (row_b == t - a) & (xpar == p), reps[3 * a + j - p], block
                        )
            wb[256 * j + 32 * i : 256 * j + 32 * i + 32] = block.astype(BF16)
    b_skip = spread(b4[1:2], t256_f)
    bias[1:2, 0:256] = jnp.where(ok_a[0:1], b_skip, 0.0)
    bias[2:3, 0:256] = jnp.where(ok_b[0:1], b_skip, 0.0)

    slots = []
    for c in range(3):
        slots += [(1, c), (2, c), (3, c), ((None, 0), (0, 2), (4, 2))[c]]
    slots += [(0, 0), (4, 0), (0, 1), (4, 1)]
    q_of = lane >> 6
    for dx in range(3):
        reps = [dot(w_coarse[3 * ca + dx], t64) for ca in range(9)]
        for i, (p, c) in enumerate(slots):
            block = zero
            if p is not None:
                for a in range(3):
                    block = jnp.where(q_of == p - a, reps[3 * c + a], block)
            wc[512 * dx + 32 * i : 512 * dx + 32 * i + 32] = block.astype(BF16)
    bias[3:4, 0:256] = spread(b_coarse[...], t64_f)

    lane64 = iota((64, 256), 1)
    quarter64 = (lane64 >> 5) & 3
    ok64 = within(y0 - 2 + 2 * quarter64 + (lane64 >> 7), full_y)
    rep = dot_tn(w_lift[...], t256)
    for q in range(3):
        wl[64 * q : 64 * q + 64] = jnp.where((quarter64 == q) & ok64, rep, 0.0).astype(BF16)
    wl[192:256] = jnp.zeros((64, 256), BF16)
    bias[4:5, 0:256] = jnp.where(ok_a[0:1], spread(b4[2:3], t256_f), 0.0)

    xi_of, f_of = lane >> 6, (lane >> 5) & 1
    reps = [dot_tn(w_final[tap], t256) for tap in range(9)]
    for j in range(6):
        for i in range(8):
            row = 2 + 2 * (i & 3) + (i >> 2)
            block = zero
            if (i & 3) < 3:
                for a in range(3):
                    for dx in range(3):
                        if 0 <= row - 3 - a < 2 and 0 <= j - dx < 4:
                            block = jnp.where(
                                (f_of == row - 3 - a) & (xi_of == j - dx), reps[3 * a + dx], block
                            )
            wf[256 * j + 32 * i : 256 * j + 32 * i + 32] = block.astype(BF16)
    bias[5:6, 0:256] = spread(b4[3:4], t256_f)

    row = iota((32, 256), 0)
    rep = dot(w_head[...], t256)
    block = zero
    for o in range(3):
        here = ((row >> 3) == xi_of) & ((row & 7) == 2 * o + f_of)
        block = jnp.where(here, rep[o : o + 1], block)
    wh[...] = block.astype(BF16)
    kind = iota((8, 512), 0)
    bias[8:16] = jnp.where(kind < 2, b_head[0], jnp.where(kind < 4, b_head[1], b_head[2]))
    for k, term in enumerate(in_three(bias[...])):
        wv[32 * k : 32 * k + 16] = term[:, 0:256]
        wv[32 * k + 16 : 32 * k + 32] = term[:, 256:512]


def prepare(pos, b_head, brick_y, full_y, pack, w_stem, w_skip, w_coarse, w_lift, w_final, w_head, b4, b_coarse):
    vmem = pl.BlockSpec(memory_space=pltpu.VMEM)
    return pl.pallas_call(
        functools.partial(prep_kernel, brick_y, full_y, pack),
        out_shape=jax.ShapeDtypeStruct((WEIGHT_ROWS, 256), BF16),
        in_specs=[pl.BlockSpec(memory_space=pltpu.SMEM)] * 2 + [vmem] * 8,
        out_specs=vmem,
        scratch_shapes=[pltpu.VMEM((16, 512), F32)],
        cost_estimate=pl.CostEstimate(
            flops=100_000_000, bytes_accessed=4_000_000, transcendentals=0
        ),
        compiler_params=pltpu.CompilerParams(vmem_limit_bytes=12 * MIB),
    )(pos, b_head, w_stem, w_skip, w_coarse, w_lift, w_final, w_head, b4, b_coarse)


def brick_kernel(
    parts_gz,
    cols,
    steps,
    pack,
    pos_ref,
    r_ref,
    packed,
    out_ref,
    bias,
    shared,
    middle,
    tmp,
    rin,
    stem,
    skip,
    pooled,
    fin,
):
    wa, wb, wc, wl, wf, wh, wv, ws, wt = parts_of(packed)
    terms = [
        jnp.concatenate([wv[32 * k : 32 * k + 16], wv[32 * k + 16 : 32 * k + 32]], axis=1)
        for k in range(3)
    ]
    bias[...] = terms[0].astype(F32) + (terms[1].astype(F32) + terms[2].astype(F32))
    nz, have = r_ref.shape[0:2]
    pitch = tmp.shape[0] // nz
    per, slots, ahead_x, _ = pack
    blocks = -(-(cols + 6 + ahead_x) // per)
    step = 0 if steps == 1 else pl.program_id(0)
    leftmost = (pos_ref[0] == 0) & (step == 0)
    rightmost = (pos_ref[0] == parts_gz - 1) & (step == steps - 1)

    def row_of(z):
        return z % (nz // 8) * 8 + z // (nz // 8)

    for z in range(nz):
        tmp[z * pitch : z * pitch + have] = r_ref[z].astype(F32)
    for b in range(blocks):
        rows = [
            tmp[pl.ds(step * (cols // 8) + b + k * pitch, 8, stride=nz // 8 * pitch), :]
            for k in range(nz // 8)
        ]
        rin[b] = jnp.concatenate(rows, axis=0).astype(BF16)

    b_stem = bias[0:1, 0:384]

    def stem_put(acc, first, i):
        out = relu(acc + b_stem).astype(BF16)
        low = iota((acc.shape[0], LANES), 1) < 64
        ends = jnp.where(low, out[:, 0:128], out[:, 128:256])
        for b in range(acc.shape[0] // nz):
            u = per * (first + b) + i + 8 - ahead_x
            stem[u >> 1, u & 1, :, 0:384] = out[b * nz : b * nz + nz]
            stem[u >> 1, u & 1, :, 384:512] = ends[b * nz : b * nz + nz]

    shared[:, 0:256] = ws[512:736].astype(F32)
    shared[0:112, 256:384] = wt[256:368, 0:128].astype(F32)
    shared[112:224, 256:384] = wt[256:368, 128:256].astype(F32)

    for i in range(per - 2):
        start = MIDDLE - slots * i
        middle[i] = shared[start : start + LANES, :].astype(BF16)

    def stem_mid(i, carry):
        stem_put(dot(rin[...].reshape(blocks * nz, LANES), middle[i - 1]), 0, i)
        return carry

    lax.fori_loop(1, per - 1, stem_mid, 0, unroll=per - 2)
    pair = jnp.concatenate([rin[0 : blocks - 1], rin[1:blocks]], axis=-1)
    pair = pair.reshape((blocks - 1) * nz, 2 * LANES)
    for part, (first, i) in enumerate(((1, 0), (0, per - 1))):
        weight = jnp.concatenate(
            [ws[256 * part : 256 * part + 256], wt[0:256, 128 * part : 128 * part + 128]], axis=1
        )
        stem_put(dot(pair, weight), first, i)

    @pl.when(leftmost)
    def _():
        stem[0:4] = jnp.zeros((4,) + stem.shape[1:], BF16)

    @pl.when(rightmost)
    def _():
        stem[cols // 2 + 4 : cols // 2 + 8] = jnp.zeros((4,) + stem.shape[1:], BF16)

    pairs = cols // 2 + 4
    mc = divisor(pairs, 2112 // nz)
    m_rows = mc * nz

    def skip_step(i, carry):
        m0 = i * mc

        def taken(u, half):
            part = stem[pl.ds(m0 + u // 2, mc), u % 2, :, 256 * half : 256 * half + 256]
            return part.reshape(m_rows, 256)

        near = [
            jnp.concatenate([taken(3 + k, 0), taken(4 + k, 0)], axis=0) for k in range(3)
        ]
        acc = dot(jnp.concatenate(near, axis=1), wa[...])
        acc = relu(acc + bias[1:2, 0:256])
        best = jnp.maximum(acc[:, 0:128], acc[:, 128:256])
        top = jnp.maximum(best[0:m_rows], best[m_rows:])
        for p in range(2):
            out = acc[p * m_rows : p * m_rows + m_rows].astype(BF16)
            skip[pl.ds(m0, mc), p] = out.reshape(mc, nz, 256)
        acc = dot(taken(3, 1), wb[0:256])
        for j in range(1, 4):
            acc += dot(taken(3 + j, 1), wb[256 * j : 256 * j + 256])
        best = jnp.maximum(acc[:, 0:128], acc[:, 128:256])
        best = jnp.maximum(best, pltpu.roll(best, 64, axis=1))
        ends = relu(best + bias[2:3, 0:128])
        lane = iota((m_rows, LANES), 1)
        sub = iota((mc, 1, 8, LANES), 2)

        def below(x):
            x = x.reshape(mc, nz // 8, 8, LANES)
            turned = jnp.where(sub == 0, 0.0, pltpu.roll(x[:, -1:], 1, axis=2))
            return jnp.concatenate([turned, x[:, :-1]], axis=1).reshape(m_rows, LANES)

        def above(x):
            x = x.reshape(mc, nz // 8, 8, LANES)
            turned = jnp.where(sub == 7, 0.0, pltpu.roll(x[:, :1], 7, axis=2))
            return jnp.concatenate([x[:, 1:], turned], axis=1).reshape(m_rows, LANES)

        ends_above = above(ends)
        parts = (
            below(top),
            jnp.where(lane < 96, top, pltpu.roll(ends_above, 32, axis=1)),
            jnp.where(lane < 96, above(top), ends_above),
            jnp.where(lane < 64, below(ends), ends),
        )
        for k in range(4):
            pooled[pl.ds(m0, mc), :, 128 * k : 128 * k + 128] = (
                parts[k].astype(BF16).reshape(mc, nz, LANES)
            )
        return carry

    lax.fori_loop(0, pairs // mc, skip_step, 0)

    @pl.when(leftmost)
    def _():
        pooled[0:2] = jnp.zeros((2,) + pooled.shape[1:], BF16)

    @pl.when(rightmost)
    def _():
        pooled[pairs - 2 : pairs] = jnp.zeros((2,) + pooled.shape[1:], BF16)

    count = cols // 2 + 2
    nc = divisor(count, 832 // nz)
    n_rows = nc * nz

    def coarse_step(i, carry):
        n0 = i * nc
        acc = dot(pooled[pl.ds(n0, nc)].reshape(n_rows, 512), wc[0:512])
        acc += dot(pooled[pl.ds(n0 + 1, nc)].reshape(n_rows, 512), wc[512:1024])
        acc += dot(pooled[pl.ds(n0 + 2, nc)].reshape(n_rows, 512), wc[1024:1536])
        coarse = relu(acc + bias[3:4, 0:256]).astype(BF16)
        lifted = dot(coarse, wl[...])
        for p in range(2):
            base = skip[pl.ds(n0 + 1, nc), p].reshape(n_rows, 256).astype(F32)
            out = relu(base + lifted + bias[4:5, 0:256]).astype(BF16)
            for k in range(nc):
                n = n0 + k
                stem[n >> 1, n & 1, :, 256 * p : 256 * p + 256] = out[k * nz : k * nz + nz]
        return carry

    lax.fori_loop(0, count // nc, coarse_step, 0)

    @pl.when(leftmost)
    def _():
        stem[0, 0] = jnp.zeros(stem.shape[2:], BF16)

    @pl.when(rightmost)
    def _():
        stem[cols // 4, 1] = jnp.zeros(stem.shape[2:], BF16)

    quads = cols // 4
    qc = divisor(quads, 1024 // nz)
    q_rows = qc * nz

    def final_step(i, carry):
        q0 = i * qc
        acc = jnp.zeros((q_rows, 256), F32)
        for j in range(6):
            k = (1 + j) % 4
            half = 256 * (k % 2)
            part = stem[pl.ds(q0 + (1 + j) // 4, qc), k // 2, :, half : half + 256]
            acc += dot(part.reshape(q_rows, 256), wf[256 * j : 256 * j + 256])
        out = relu(acc + bias[5:6, 0:256])
        for k in range(2):
            fin[k, pl.ds(pl.multiple_of(q0 * nz, 8), q_rows), :] = out[:, 128 * k : 128 * k + 128]
        return carry

    lax.fori_loop(0, quads // qc, final_step, 0)

    together = LANES // quads
    groups = nz // together
    lines = []
    for g in range(groups):
        sides = []
        for side in range(2):
            rows = [
                fin[side, pl.ds(row_of(g * together + k), quads, stride=nz), :]
                for k in range(together)
            ]
            sides.append(jnp.concatenate(rows, axis=0).astype(BF16))
        h = dot_nt(wh[...], jnp.concatenate(sides, axis=1))
        lines.append(jnp.concatenate([h[8 * xi : 8 * xi + 8] for xi in range(4)], axis=1))
    table = jnp.concatenate(lines, axis=0)
    size = together * cols
    row = iota((512, size), 0)
    order = jnp.where(iota((512, size), 1) == 4 * (row & 127) + (row >> 7), 1.0, 0.0).astype(BF16)
    high, middle, low = in_three(table)
    result = dot(high, order) + (dot(middle, order) + dot(low, order))
    result = result.reshape(groups, 8, size) + bias[8:16, 0:size]
    for g in range(groups):
        for k in range(together):
            for o in range(3):
                out_ref[o, g * together + k] = (
                    result[g, 2 * o : 2 * o + 2, k * cols : k * cols + cols]
                )


def brick(pos, received, weights, parts_gz, brick_y, brick_x):
    nz, have = received.shape[0:2]
    cols, pack = chunk(brick_x, nz), packing(brick_x, nz)
    steps = brick_x // cols
    scratch = [
        ((16, 512), F32),
        ((224, 384), F32),
        ((pack[0] - 2, LANES, 384), BF16),
        ((nz * round_up(have, 8), LANES), F32),
        ((-(-(cols + 6 + pack[2]) // pack[0]), nz, LANES), BF16),
        ((cols // 2 + 8, 2, nz, 512), BF16),
        ((cols // 2 + 4, 2, nz, 256), BF16),
        ((cols // 2 + 4, nz, 512), BF16),
        ((2, cols // 4 * nz, LANES), F32),
    ]
    operands = [(received.shape, BF16), (weights.shape, BF16), ((6, nz, 8, cols), F32)]
    held = sum(math.prod(shape) * jnp.dtype(dtype).itemsize for shape, dtype in scratch + operands)
    vmem = pl.BlockSpec(memory_space=pltpu.VMEM)
    smem = pl.BlockSpec(memory_space=pltpu.SMEM)
    return pl.pallas_call(
        functools.partial(brick_kernel, parts_gz, cols, steps, pack),
        grid=(steps,),
        out_shape=jax.ShapeDtypeStruct((3, nz, brick_y, brick_x), F32),
        in_specs=[smem, vmem, vmem],
        out_specs=pl.BlockSpec((3, nz, brick_y, cols), lambda i: (0, 0, 0, i)),
        scratch_shapes=[pltpu.VMEM(shape, dtype) for shape, dtype in scratch],
        cost_estimate=pl.CostEstimate(
            flops=20_000_000_000, bytes_accessed=4_000_000, transcendentals=0
        ),
        compiler_params=pltpu.CompilerParams(vmem_limit_bytes=min(held + 6 * MIB, 60 * MIB)),
    )(pos, received, weights)


def local(
    image,
    offsets,
    w_stem,
    b_stem,
    w_skip,
    b_skip,
    w_coarse,
    b_coarse,
    w_lift,
    b_lift,
    w_final,
    b_final,
    w_head,
    b_head,
):
    parts_gz, parts_gy = lax.axis_size("gz"), lax.axis_size("gy")
    full_y, full_x = image.shape[1:]
    brick_y, brick_x = full_y // parts_gy, full_x // parts_gz
    assert image.shape[0] == 1 and brick_y == 2
    pos = jnp.stack([lax.axis_index("gz"), lax.axis_index("gy")]).astype(I32)
    nz = parts_gz * parts_gy
    windows = make_windows(image, offsets, parts_gz, parts_gy, nz)
    received = lax.all_to_all(windows, ("gz", "gy"), 0, 0, tiled=True)
    b4 = jnp.stack([b_stem, b_skip, b_lift, b_final])
    weights = prepare(
        pos,
        b_head,
        brick_y,
        full_y,
        packing(brick_x, nz),
        w_stem.reshape(w_stem.shape[0:2]),
        w_skip,
        w_coarse.transpose(0, 2, 1),
        w_lift,
        w_final,
        w_head,
        b4,
        b_coarse[None],
    )
    return brick(pos, received, weights, parts_gz, brick_y, brick_x)


def solution(mesh):
    split = P(("gz", "gy"))
    return jax.shard_map(
        local,
        mesh=mesh,
        in_specs=(split, split) + (P(),) * 12,
        out_specs=P(None, None, "gy", "gz"),
        check_vma=False,
    )
```

```python
import functools
import math

import jax
import jax.numpy as jnp
from jax import lax
from jax.experimental import pallas as pl
from jax.experimental.pallas import tpu as pltpu
from jax.sharding import PartitionSpec as P

MAXOFF = 32
LANES = 128
PAD = MAXOFF + 8
BF16, F32, I32 = jnp.bfloat16, jnp.float32, jnp.int32
MIB = 1024 * 1024


def packing(brick_x, nz):
    return (9, 14, 6, 6) if chunk(brick_x, nz) == brick_x else (8, 16, 8, 7)


def chunk(brick_x, nz):
    cols = brick_x
    while cols * nz > 16384 and cols % 256 == 0:
        cols //= 2
    return cols


def iota(shape, dim):
    return lax.broadcasted_iota(I32, shape, dim)


def dot(a, b):
    return jnp.dot(a, b, preferred_element_type=F32)


def dot_tn(a, b):
    return lax.dot_general(a, b, (((0,), (0,)), ((), ())), preferred_element_type=F32)


def dot_nt(a, b):
    return lax.dot_general(a, b, (((1,), (1,)), ((), ())), preferred_element_type=F32)


def relu(x):
    return jnp.maximum(x, 0.0)


def round_up(n, m):
    return -(-n // m) * m


def divisor(count, most):
    return max(d for d in range(1, count + 1) if count % d == 0 and d <= max(most, 1))


def send_kernel(parts_gz, parts_gy, brick_y, brick_x, pack, off_ref, image_ref, send_ref, tall_ref):
    count, slots, ahead_x, ahead_y = pack
    full_y, full_x = image_ref.shape[1:]
    rows = send_ref.shape[1]
    off_y, off_x = off_ref[0, 0], off_ref[0, 1]
    tall_ref[...] = jnp.zeros_like(tall_ref)
    tall_ref[PAD : PAD + full_x, 0:full_y] = image_ref[0].astype(F32).T
    lane = iota((rows, LANES), 1)
    slot = lane
    for i in range(1, count):
        slot = jnp.where(lane >= slots * i, lane - slots * i, slot)
    block = iota((rows, LANES), 0) * count
    parts = -(-full_y // slots)
    for gz in range(parts_gz):
        packed = [jnp.zeros((rows, LANES), F32) for _ in range(parts)]
        for i in range(count):
            x = gz * brick_x - ahead_x + i
            column = tall_ref[pl.ds(PAD + x - off_x, rows, stride=count), :]
            here = (lane >= slots * i) & (lane < slots * i + slots)
            here &= (block >= -x) & (block < full_x - x)
            for h in range(parts):
                turn = lax.rem(off_y + (slots * (i - h) + 2 * LANES), LANES)
                turned = pltpu.roll(column, turn, axis=1)
                packed[h] = jnp.where(here & (slot < full_y - slots * h), turned, packed[h])
        for gy in range(parts_gy):
            window = jnp.zeros((rows, LANES), F32)
            for h in range(parts):
                shift = brick_y * gy - ahead_y - slots * h
                if -slots < shift < slots:
                    turned = packed[h]
                    if shift:
                        turned = pltpu.roll(turned, (-shift) % LANES, axis=1)
                    inside = (slot + shift >= 0) & (slot + shift < slots)
                    window = jnp.where(inside, turned, window)
            send_ref[gz * parts_gy + gy] = window.astype(BF16)


def make_windows(image, offsets, parts_gz, parts_gy, nz):
    full_y, full_x = image.shape[1:]
    brick_y, brick_x = full_y // parts_gy, full_x // parts_gz
    pack = packing(brick_x, nz)
    rows = round_up(-(-(brick_x + 6 + pack[2]) // pack[0]), 8)
    tall = round_up(PAD + full_x - brick_x + MAXOFF + pack[0] * rows, 8)
    return pl.pallas_call(
        functools.partial(send_kernel, parts_gz, parts_gy, brick_y, brick_x, pack),
        out_shape=jax.ShapeDtypeStruct((parts_gz * parts_gy, rows, LANES), BF16),
        in_specs=[
            pl.BlockSpec(memory_space=pltpu.SMEM),
            pl.BlockSpec(memory_space=pltpu.VMEM),
        ],
        out_specs=pl.BlockSpec(memory_space=pltpu.VMEM),
        scratch_shapes=[pltpu.VMEM((tall, LANES), F32)],
    )(offsets, image)


ENDS = (0, 1, 10, 11, 2, 3, 8, 9)


SIZES = {"a": 768, "b": 1024, "c": 1536, "l": 256, "f": 1536, "h": 32, "v": 96, "s": 736, "t": 368}
STARTS = dict(zip(SIZES, [sum(list(SIZES.values())[:k]) for k in range(len(SIZES))]))
MIDDLE = 96
WEIGHT_ROWS = sum(SIZES.values())


def parts_of(ref):
    return [ref.at[STARTS[k] : STARTS[k] + SIZES[k]] for k in SIZES]


def in_three(x):
    high = x.astype(BF16)
    rest = x - high.astype(F32)
    middle = rest.astype(BF16)
    return high, middle, (rest - middle.astype(F32)).astype(BF16)


def stem_row(s):
    return jnp.where(s < 8, s + 2, jnp.where(s < 10, s - 8, s))


def within(y, full_y):
    return (y >= 0) & (y < full_y)


def prep_kernel(
    brick_y,
    full_y,
    pack,
    pos_ref,
    b_head,
    w_stem,
    w_skip,
    w_coarse,
    w_lift,
    w_final,
    w_head,
    b4,
    b_coarse,
    packed,
    bias,
):
    wa, wb, wc, wl, wf, wh, wv, ws, wt = parts_of(packed)
    y0 = pos_ref[1] * brick_y
    zero = jnp.zeros((32, 256), F32)

    def tiles(count, width):
        return jnp.where((iota((count, width), 1) & (count - 1)) == iota((count, width), 0), 1.0, 0.0)

    t384_f, t256_f, t64_f = tiles(32, 384), tiles(32, 256), tiles(64, 256)
    t384, t256, t64 = t384_f.astype(BF16), t256_f.astype(BF16), t64_f.astype(BF16)

    def spread(row, table):
        return jnp.dot(row, table, precision=lax.Precision.HIGHEST, preferred_element_type=F32)

    lane = iota((1, 384), 1)
    t_of = stem_row(lane >> 5)
    stem_ok = within(y0 - 5 + t_of, full_y)
    rep = dot(w_stem[...], t384)
    lane16 = iota((16, 384), 1)
    t16 = stem_row(lane16 >> 5)
    tap16 = iota((16, 384), 0) - t16
    ok16 = within(y0 - 5 + t16, full_y)
    taps = []
    for dx in range(3):
        block = jnp.zeros((16, 384), F32)
        for a in range(3):
            block = jnp.where((tap16 == a) & ok16, rep[3 * a + dx : 3 * a + dx + 1], block)
        taps.append(block)
    taps = jnp.concatenate(taps, axis=0).astype(BF16)
    count, slots, _, ahead_y = pack
    for part, i in enumerate((0, count - 1, None)):
        depth = 256 if part < 2 else 224
        row, column = iota((depth, 48), 0), iota((depth, 48), 1)
        place = jnp.zeros((depth, 48), F32)
        for dx in range(3):
            if part < 2:
                at = i - 1 + dx
                start = slots * (at % count) + 128 * (at // count + (i == 0))
            else:
                start = MIDDLE + slots * dx
            near = (column >= 16 * dx) & (column < 16 * dx + 14)
            here = row == start + ahead_y - 6 + column - 16 * dx
            place = jnp.where(near & here, 1.0, place)
        block = dot(place.astype(BF16), taps).astype(BF16)
        ws[256 * part : 256 * part + depth] = block[:, 0:256]
        if part < 2:
            wt[0:256, 128 * part : 128 * part + 128] = block[:, 256:384]
        else:
            wt[256:368, 0:128] = block[0:112, 256:384]
            wt[256:368, 128:256] = block[112:224, 256:384]
    bias[...] = jnp.zeros_like(bias)
    bias[0:1, 0:384] = jnp.where(stem_ok, spread(b4[0:1], t384_f), 0.0)

    lane = iota((32, 256), 1)
    half, quarter = lane >> 7, (lane >> 5) & 3
    row_a = 2 + 2 * quarter + half
    ok_a = (quarter < 3) & within(y0 - 4 + row_a, full_y)
    row_a = jnp.where(ok_a, row_a, -99)
    xpar = quarter >> 1
    row_b = 8 * (quarter & 1) + half
    ok_b = within(y0 - 4 + row_b, full_y)
    row_b = jnp.where(ok_b, row_b, -99)
    reps = [dot_tn(w_skip[tap], t256) for tap in range(9)]
    for dx in range(3):
        for i in range(8):
            block = zero
            for a in range(3):
                block = jnp.where(row_a == 2 + i - a, reps[3 * a + dx], block)
            wa[256 * dx + 32 * i : 256 * dx + 32 * i + 32] = block.astype(BF16)
    for j in range(4):
        for i in range(8):
            t = ENDS[i]
            block = zero
            for a in range(3):
                for p in range(2):
                    if 0 <= j - p < 3:
                        block = jnp.where(
                            (row_b == t - a) & (xpar == p), reps[3 * a + j - p], block
                        )
            wb[256 * j + 32 * i : 256 * j + 32 * i + 32] = block.astype(BF16)
    b_skip = spread(b4[1:2], t256_f)
    bias[1:2, 0:256] = jnp.where(ok_a[0:1], b_skip, 0.0)
    bias[2:3, 0:256] = jnp.where(ok_b[0:1], b_skip, 0.0)

    slots = []
    for c in range(3):
        slots += [(1, c), (2, c), (3, c), ((None, 0), (0, 2), (4, 2))[c]]
    slots += [(0, 0), (4, 0), (0, 1), (4, 1)]
    q_of = lane >> 6
    for dx in range(3):
        reps = [dot(w_coarse[3 * ca + dx], t64) for ca in range(9)]
        for i, (p, c) in enumerate(slots):
            block = zero
            if p is not None:
                for a in range(3):
                    block = jnp.where(q_of == p - a, reps[3 * c + a], block)
            wc[512 * dx + 32 * i : 512 * dx + 32 * i + 32] = block.astype(BF16)
    bias[3:4, 0:256] = spread(b_coarse[...], t64_f)

    lane64 = iota((64, 256), 1)
    quarter64 = (lane64 >> 5) & 3
    ok64 = within(y0 - 2 + 2 * quarter64 + (lane64 >> 7), full_y)
    rep = dot_tn(w_lift[...], t256)
    for q in range(3):
        wl[64 * q : 64 * q + 64] = jnp.where((quarter64 == q) & ok64, rep, 0.0).astype(BF16)
    wl[192:256] = jnp.zeros((64, 256), BF16)
    bias[4:5, 0:256] = jnp.where(ok_a[0:1], spread(b4[2:3], t256_f), 0.0)

    xi_of, f_of = lane >> 6, (lane >> 5) & 1
    reps = [dot_tn(w_final[tap], t256) for tap in range(9)]
    for j in range(6):
        for i in range(8):
            row = 2 + 2 * (i & 3) + (i >> 2)
            block = zero
            if (i & 3) < 3:
                for a in range(3):
                    for dx in range(3):
                        if 0 <= row - 3 - a < 2 and 0 <= j - dx < 4:
                            block = jnp.where(
                                (f_of == row - 3 - a) & (xi_of == j - dx), reps[3 * a + dx], block
                            )
            wf[256 * j + 32 * i : 256 * j + 32 * i + 32] = block.astype(BF16)
    bias[5:6, 0:256] = spread(b4[3:4], t256_f)

    row = iota((32, 256), 0)
    rep = dot(w_head[...], t256)
    block = zero
    for o in range(3):
        here = ((row >> 3) == xi_of) & ((row & 7) == 2 * o + f_of)
        block = jnp.where(here, rep[o : o + 1], block)
    wh[...] = block.astype(BF16)
    kind = iota((8, 512), 0)
    bias[8:16] = jnp.where(kind < 2, b_head[0], jnp.where(kind < 4, b_head[1], b_head[2]))
    for k, term in enumerate(in_three(bias[...])):
        wv[32 * k : 32 * k + 16] = term[:, 0:256]
        wv[32 * k + 16 : 32 * k + 32] = term[:, 256:512]


def prepare(pos, b_head, brick_y, full_y, pack, w_stem, w_skip, w_coarse, w_lift, w_final, w_head, b4, b_coarse):
    vmem = pl.BlockSpec(memory_space=pltpu.VMEM)
    return pl.pallas_call(
        functools.partial(prep_kernel, brick_y, full_y, pack),
        out_shape=jax.ShapeDtypeStruct((WEIGHT_ROWS, 256), BF16),
        in_specs=[pl.BlockSpec(memory_space=pltpu.SMEM)] * 2 + [vmem] * 8,
        out_specs=vmem,
        scratch_shapes=[pltpu.VMEM((16, 512), F32)],
        cost_estimate=pl.CostEstimate(
            flops=100_000_000, bytes_accessed=4_000_000, transcendentals=0
        ),
        compiler_params=pltpu.CompilerParams(vmem_limit_bytes=12 * MIB),
    )(pos, b_head, w_stem, w_skip, w_coarse, w_lift, w_final, w_head, b4, b_coarse)


def brick_kernel(
    parts_gz,
    cols,
    steps,
    pack,
    pos_ref,
    r_ref,
    packed,
    out_ref,
    bias,
    shared,
    middle,
    tmp,
    rin,
    stem,
    skip,
    pooled,
    fin,
):
    wa, wb, wc, wl, wf, wh, wv, ws, wt = parts_of(packed)
    terms = [
        jnp.concatenate([wv[32 * k : 32 * k + 16], wv[32 * k + 16 : 32 * k + 32]], axis=1)
        for k in range(3)
    ]
    bias[...] = terms[0].astype(F32) + (terms[1].astype(F32) + terms[2].astype(F32))
    nz, have = r_ref.shape[0:2]
    pitch = tmp.shape[0] // nz
    per, slots, ahead_x, _ = pack
    blocks = -(-(cols + 6 + ahead_x) // per)
    step = 0 if steps == 1 else pl.program_id(0)
    leftmost = (pos_ref[0] == 0) & (step == 0)
    rightmost = (pos_ref[0] == parts_gz - 1) & (step == steps - 1)

    def row_of(z):
        return z % (nz // 8) * 8 + z // (nz // 8)

    for z in range(nz):
        tmp[z * pitch : z * pitch + have] = r_ref[z].astype(F32)
    for b in range(blocks):
        rows = [
            tmp[pl.ds(step * (cols // 8) + b + k * pitch, 8, stride=nz // 8 * pitch), :]
            for k in range(nz // 8)
        ]
        rin[b] = jnp.concatenate(rows, axis=0).astype(BF16)

    b_stem = bias[0:1, 0:384]

    def stem_put(acc, first, i):
        out = relu(acc + b_stem).astype(BF16)
        low = iota((acc.shape[0], LANES), 1) < 64
        ends = jnp.where(low, out[:, 0:128], out[:, 128:256])
        for b in range(acc.shape[0] // nz):
            u = per * (first + b) + i + 8 - ahead_x
            stem[u >> 1, u & 1, :, 0:384] = out[b * nz : b * nz + nz]
            stem[u >> 1, u & 1, :, 384:512] = ends[b * nz : b * nz + nz]

    shared[:, 0:256] = ws[512:736].astype(F32)
    shared[0:112, 256:384] = wt[256:368, 0:128].astype(F32)
    shared[112:224, 256:384] = wt[256:368, 128:256].astype(F32)

    for i in range(per - 2):
        start = MIDDLE - slots * i
        middle[i] = shared[start : start + LANES, :].astype(BF16)

    def stem_mid(i, carry):
        stem_put(dot(rin[...].reshape(blocks * nz, LANES), middle[i - 1]), 0, i)
        return carry

    lax.fori_loop(1, per - 1, stem_mid, 0, unroll=per - 2)
    pair = jnp.concatenate([rin[0 : blocks - 1], rin[1:blocks]], axis=-1)
    pair = pair.reshape((blocks - 1) * nz, 2 * LANES)
    for part, (first, i) in enumerate(((1, 0), (0, per - 1))):
        weight = jnp.concatenate(
            [ws[256 * part : 256 * part + 256], wt[0:256, 128 * part : 128 * part + 128]], axis=1
        )
        stem_put(dot(pair, weight), first, i)

    @pl.when(leftmost)
    def _():
        stem[0:4] = jnp.zeros((4,) + stem.shape[1:], BF16)

    @pl.when(rightmost)
    def _():
        stem[cols // 2 + 4 : cols // 2 + 8] = jnp.zeros((4,) + stem.shape[1:], BF16)

    pairs = cols // 2 + 4
    mc = divisor(pairs, 2112 // nz)
    m_rows = mc * nz

    def skip_step(i, carry):
        m0 = i * mc

        def taken(u, half):
            part = stem[pl.ds(m0 + u // 2, mc), u % 2, :, 256 * half : 256 * half + 256]
            return part.reshape(m_rows, 256)

        near = [
            jnp.concatenate([taken(3 + k, 0), taken(4 + k, 0)], axis=0) for k in range(3)
        ]
        acc = dot(jnp.concatenate(near, axis=1), wa[...])
        acc = relu(acc + bias[1:2, 0:256])
        best = jnp.maximum(acc[:, 0:128], acc[:, 128:256])
        top = jnp.maximum(best[0:m_rows], best[m_rows:])
        for p in range(2):
            out = acc[p * m_rows : p * m_rows + m_rows].astype(BF16)
            skip[pl.ds(m0, mc), p] = out.reshape(mc, nz, 256)
        acc = dot(taken(3, 1), wb[0:256])
        for j in range(1, 4):
            acc += dot(taken(3 + j, 1), wb[256 * j : 256 * j + 256])
        best = jnp.maximum(acc[:, 0:128], acc[:, 128:256])
        best = jnp.maximum(best, pltpu.roll(best, 64, axis=1))
        ends = relu(best + bias[2:3, 0:128])
        lane = iota((m_rows, LANES), 1)
        sub = iota((mc, 1, 8, LANES), 2)

        def below(x):
            x = x.reshape(mc, nz // 8, 8, LANES)
            turned = jnp.where(sub == 0, 0.0, pltpu.roll(x[:, -1:], 1, axis=2))
            return jnp.concatenate([turned, x[:, :-1]], axis=1).reshape(m_rows, LANES)

        def above(x):
            x = x.reshape(mc, nz // 8, 8, LANES)
            turned = jnp.where(sub == 7, 0.0, pltpu.roll(x[:, :1], 7, axis=2))
            return jnp.concatenate([x[:, 1:], turned], axis=1).reshape(m_rows, LANES)

        ends_above = above(ends)
        parts = (
            below(top),
            jnp.where(lane < 96, top, pltpu.roll(ends_above, 32, axis=1)),
            jnp.where(lane < 96, above(top), ends_above),
            jnp.where(lane < 64, below(ends), ends),
        )
        for k in range(4):
            pooled[pl.ds(m0, mc), :, 128 * k : 128 * k + 128] = (
                parts[k].astype(BF16).reshape(mc, nz, LANES)
            )
        return carry

    lax.fori_loop(0, pairs // mc, skip_step, 0)

    @pl.when(leftmost)
    def _():
        pooled[0:2] = jnp.zeros((2,) + pooled.shape[1:], BF16)

    @pl.when(rightmost)
    def _():
        pooled[pairs - 2 : pairs] = jnp.zeros((2,) + pooled.shape[1:], BF16)

    count = cols // 2 + 2
    nc = divisor(count, 2080 // nz)
    n_rows = nc * nz

    def coarse_step(i, carry):
        n0 = i * nc
        acc = dot(pooled[pl.ds(n0, nc)].reshape(n_rows, 512), wc[0:512])
        acc += dot(pooled[pl.ds(n0 + 1, nc)].reshape(n_rows, 512), wc[512:1024])
        acc += dot(pooled[pl.ds(n0 + 2, nc)].reshape(n_rows, 512), wc[1024:1536])
        coarse = relu(acc + bias[3:4, 0:256]).astype(BF16)
        lifted = dot(coarse, wl[...])
        for p in range(2):
            base = skip[pl.ds(n0 + 1, nc), p].reshape(n_rows, 256).astype(F32)
            out = relu(base + lifted + bias[4:5, 0:256]).astype(BF16)
            for k in range(nc):
                n = n0 + k
                stem[n >> 1, n & 1, :, 256 * p : 256 * p + 256] = out[k * nz : k * nz + nz]
        return carry

    lax.fori_loop(0, count // nc, coarse_step, 0)

    @pl.when(leftmost)
    def _():
        stem[0, 0] = jnp.zeros(stem.shape[2:], BF16)

    @pl.when(rightmost)
    def _():
        stem[cols // 4, 1] = jnp.zeros(stem.shape[2:], BF16)

    quads = cols // 4
    qc = divisor(quads, 1024 // nz)
    q_rows = qc * nz

    def final_step(i, carry):
        q0 = i * qc
        acc = jnp.zeros((q_rows, 256), F32)
        for j in range(6):
            k = (1 + j) % 4
            half = 256 * (k % 2)
            part = stem[pl.ds(q0 + (1 + j) // 4, qc), k // 2, :, half : half + 256]
            acc += dot(part.reshape(q_rows, 256), wf[256 * j : 256 * j + 256])
        out = relu(acc + bias[5:6, 0:256])
        for k in range(2):
            fin[k, pl.ds(pl.multiple_of(q0 * nz, 8), q_rows), :] = out[:, 128 * k : 128 * k + 128]
        return carry

    lax.fori_loop(0, quads // qc, final_step, 0)

    together = LANES // quads
    groups = nz // together
    lines = []
    for g in range(groups):
        sides = []
        for side in range(2):
            rows = [
                fin[side, pl.ds(row_of(g * together + k), quads, stride=nz), :]
                for k in range(together)
            ]
            sides.append(jnp.concatenate(rows, axis=0).astype(BF16))
        h = dot_nt(wh[...], jnp.concatenate(sides, axis=1))
        lines.append(jnp.concatenate([h[8 * xi : 8 * xi + 8] for xi in range(4)], axis=1))
    table = jnp.concatenate(lines, axis=0)
    size = together * cols
    row = iota((512, size), 0)
    order = jnp.where(iota((512, size), 1) == 4 * (row & 127) + (row >> 7), 1.0, 0.0).astype(BF16)
    high, middle, low = in_three(table)
    result = dot(high, order) + (dot(middle, order) + dot(low, order))
    result = result.reshape(groups, 8, size) + bias[8:16, 0:size]
    for g in range(groups):
        for k in range(together):
            for o in range(3):
                out_ref[o, g * together + k] = (
                    result[g, 2 * o : 2 * o + 2, k * cols : k * cols + cols]
                )


def brick(pos, received, weights, parts_gz, brick_y, brick_x):
    nz, have = received.shape[0:2]
    cols, pack = chunk(brick_x, nz), packing(brick_x, nz)
    steps = brick_x // cols
    scratch = [
        ((16, 512), F32),
        ((224, 384), F32),
        ((pack[0] - 2, LANES, 384), BF16),
        ((nz * round_up(have, 8), LANES), F32),
        ((-(-(cols + 6 + pack[2]) // pack[0]), nz, LANES), BF16),
        ((cols // 2 + 8, 2, nz, 512), BF16),
        ((cols // 2 + 4, 2, nz, 256), BF16),
        ((cols // 2 + 4, nz, 512), BF16),
        ((2, cols // 4 * nz, LANES), F32),
    ]
    operands = [(received.shape, BF16), (weights.shape, BF16), ((6, nz, 8, cols), F32)]
    held = sum(math.prod(shape) * jnp.dtype(dtype).itemsize for shape, dtype in scratch + operands)
    vmem = pl.BlockSpec(memory_space=pltpu.VMEM)
    smem = pl.BlockSpec(memory_space=pltpu.SMEM)
    return pl.pallas_call(
        functools.partial(brick_kernel, parts_gz, cols, steps, pack),
        grid=(steps,),
        out_shape=jax.ShapeDtypeStruct((3, nz, brick_y, brick_x), F32),
        in_specs=[smem, vmem, vmem],
        out_specs=pl.BlockSpec((3, nz, brick_y, cols), lambda i: (0, 0, 0, i)),
        scratch_shapes=[pltpu.VMEM(shape, dtype) for shape, dtype in scratch],
        cost_estimate=pl.CostEstimate(
            flops=20_000_000_000, bytes_accessed=4_000_000, transcendentals=0
        ),
        compiler_params=pltpu.CompilerParams(vmem_limit_bytes=min(held + 6 * MIB, 60 * MIB)),
    )(pos, received, weights)


def local(
    image,
    offsets,
    w_stem,
    b_stem,
    w_skip,
    b_skip,
    w_coarse,
    b_coarse,
    w_lift,
    b_lift,
    w_final,
    b_final,
    w_head,
    b_head,
):
    parts_gz, parts_gy = lax.axis_size("gz"), lax.axis_size("gy")
    full_y, full_x = image.shape[1:]
    brick_y, brick_x = full_y // parts_gy, full_x // parts_gz
    assert image.shape[0] == 1 and brick_y == 2
    pos = jnp.stack([lax.axis_index("gz"), lax.axis_index("gy")]).astype(I32)
    nz = parts_gz * parts_gy
    windows = make_windows(image, offsets, parts_gz, parts_gy, nz)
    received = lax.all_to_all(windows, ("gz", "gy"), 0, 0, tiled=True)
    b4 = jnp.stack([b_stem, b_skip, b_lift, b_final])
    weights = prepare(
        pos,
        b_head,
        brick_y,
        full_y,
        packing(brick_x, nz),
        w_stem.reshape(w_stem.shape[0:2]),
        w_skip,
        w_coarse.transpose(0, 2, 1),
        w_lift,
        w_final,
        w_head,
        b4,
        b_coarse[None],
    )
    return brick(pos, received, weights, parts_gz, brick_y, brick_x)


def solution(mesh):
    split = P(("gz", "gy"))
    return jax.shard_map(
        local,
        mesh=mesh,
        in_specs=(split, split) + (P(),) * 12,
        out_specs=P(None, None, "gy", "gz"),
        check_vma=False,
    )
```
